32 devices in a mesh: tile: 16 (over z, x, core), tm: 2 (over y).
Axes of the slice: x: 2, y: 2, z: 4, core: 2. Of those that a mesh axis runs over, the one named last changes fastest.
Arguments:
- data: bfloat16 [2048, 16, 128], P('tile', 'tm'), may hold values from -8 to 8
- send_list: int32 [16, 16, 8], P('tile'), may hold values from 0 to 127
- footprint_slot: int32 [2048, 8], P('tile'), may hold values from 0 to 127, as said below
- footprint: bfloat16 [2048, 8, 128], P('tile'), may hold values from 0 to 0.053955078
- colour: int32 [2048], P('tile'), may hold values from 0 to 3, as said below
- correlation: int32 [2048, 8], P('tile'), may hold values from 0 to 2047, as said below
- correlation_gram: float32 [2048, 8], P('tile'), may hold values from 0.01 to 0.15
- traces_init: float32 [16, 2048], P('tm', 'tile'), may hold values from 0 to 4
Outputs:
- traces: float32 [16, 2048], P('tm', 'tile')
- trace_rms: float32 [2048], P('tile')
The draws below stay inside these ranges and needn't reach their ends.
Inputs may be any that keep to these rules, and one draw needn't show every extreme that they name: footprint_slot[k, j] names the slot c = footprint_slot[k, j] % 8 in which tile device footprint_slot[k, j] // 8 sends a block to the owner of k, tile device k // 128; the 8 slots of one footprint differ. Each tile device owns exactly a quarter of its 128 components in each colour; every listed neighbour has a colour other than the component's own. `correlation`: the tile axis folds the slab's two halves end to end, so the neighbours of a component owned by tile device d are owned by tile device d - 1, d, d + 1 or (d + 8) modulo 16; entries may repeat.
All inputs are finite; a program needn't handle non-finite values.
Results may differ from the reference program's by a relative error of at most 0.0003.
Values may be sent and summed in bfloat16 or wider, within the bound.
No kernel may reach another device: no remote copies, remote signals or barrier semaphores. Data moves between devices by JAX's collectives and lax.ppermute only.
A program may use at most 64 MiB of HBM per device.

```python
import math
import jax
import jax.numpy as jnp
from jax import lax

VOX = 128
VB_DEV = 128
K_DEV = 128
FPB = 8
CAP = 8
OV = 8
NBLK = 2048
FRAMES = 16
K = 2048
SLOTS = 128
N_TILE = 16


def colour_plan(key):
    tiles_all = K // K_DEV
    quarter = K_DEV // 4
    scores = jax.random.randint(jax.random.fold_in(key, 1), (tiles_all, K_DEV), 0, 2 ** 20)
    scores = scores * K_DEV + jnp.arange(K_DEV, dtype=jnp.int32)[None, :]
    sorted_index = jnp.argsort(scores, axis=1).astype(jnp.int32)
    positions = jnp.argsort(sorted_index, axis=1).astype(jnp.int32)
    colours = (positions % 4).reshape(K)
    owner_dev = jnp.arange(K, dtype=jnp.int32) // K_DEV
    offsets = jax.random.randint(jax.random.fold_in(key, 2), (K, OV), -1, 2)
    near_target = jnp.clip(owner_dev[:, None] + offsets, 0, tiles_all - 1)
    far_target = (owner_dev[:, None] + tiles_all // 2) % tiles_all
    column_ids = jnp.arange(OV, dtype=jnp.int32)[None, :]
    target = jnp.where(column_ids == OV - 1, far_target, near_target)
    shifts = jax.random.randint(jax.random.fold_in(key, 3), (K, OV), 1, 4)
    wanted = (colours[:, None] + shifts) % 4
    member = jax.random.randint(jax.random.fold_in(key, 4), (K, OV), 0, quarter)
    local_index = sorted_index[target, 4 * member + wanted]
    neighbour_ids = target * K_DEV + local_index
    return (colours.astype(jnp.int32), neighbour_ids.astype(jnp.int32))


def draw_colour(key, part):
    return colour_plan(jax.random.fold_in(key, 7))[0]


def draw_correlation(key, part):
    return colour_plan(jax.random.fold_in(key, 7))[1]


def draw_footprint_slot(key, part):
    band_size = SLOTS // FPB
    picked = jax.random.randint(key, (K, FPB), 0, band_size)
    return (picked + jnp.arange(FPB, dtype=jnp.int32)[None, :] * band_size).astype(jnp.int32)


def draw_data(key, part):
    first_key, second_key = jax.random.split(key)
    frame_pos = jnp.arange(FRAMES, dtype=jnp.float32)
    bleach = jnp.exp(-1.2 * frame_pos / FRAMES)[None, :, None]
    bright = jax.random.uniform(first_key, (NBLK, 1, 1), jnp.float32, 0.5, 2.0)
    noise = jax.random.truncated_normal(second_key, -3.5, 3.5, (NBLK, FRAMES, VOX), jnp.float32)
    return (bleach * bright * (0.1 + noise)).astype(jnp.bfloat16)


def place_ends(result, own_key, smallest, high):
    dims = result.shape
    place = [jax.random.randint(jax.random.fold_in(own_key, axis), (), 0, dims[axis]) for axis in range(len(dims))]
    result = result.at[tuple(place)].set(smallest)
    longest = dims.index(max(dims))
    place[longest] = (place[longest] + 1) % dims[longest]
    return result.at[tuple(place)].set(high)


def levels(rng, shape, cuts, least, top_value):
    loudness = 1.0
    for axis_at, shards_of in cuts:
        heights = jax.random.uniform(jax.random.fold_in(jax.random.fold_in(rng, 6), axis_at), (shards_of,), jnp.float32, least / len(cuts), top_value / len(cuts))
        loudness = loudness * jnp.repeat(jnp.exp(heights), shape[axis_at] // shards_of).reshape((-1,) + (1,) * (len(shape) - 1 - axis_at))
    return loudness


def setup_inputs(seed: int = 0) -> dict:
    splits = jax.random.split(jax.random.key(seed), 9)
    return {
        "data": draw_data(jax.random.fold_in(splits[8], 71), 0),
        "send_list": place_ends(jax.random.randint(splits[1], (N_TILE, N_TILE, CAP), 0, VB_DEV), jax.random.fold_in(splits[1], 1), 0, VB_DEV - 1).astype(jnp.int32),
        "footprint_slot": draw_footprint_slot(jax.random.fold_in(splits[8], 71), 0),
        "footprint": jnp.clip(0.053955078 * jax.random.uniform(splits[3], (K, FPB, VOX), jnp.float32) ** levels(splits[3], (K, FPB, VOX), ((0, 16),), -0.2, 0.2), 0.0, 0.053955078).astype(jnp.bfloat16),
        "colour": draw_colour(jax.random.fold_in(splits[8], 71), 0),
        "correlation": draw_correlation(jax.random.fold_in(splits[8], 71), 0),
        "correlation_gram": jnp.clip(jnp.exp(math.log(0.15) - 2.7080503 * jax.random.uniform(splits[6], (K, OV), jnp.float32) ** levels(splits[6], (K, OV), ((0, 16),), -0.2, 0.2)), 0.01, 0.15),
        "traces_init": jnp.clip(4.0 * jax.random.uniform(splits[7], (FRAMES, K), jnp.float32) ** levels(splits[7], (FRAMES, K), ((0, 2), (1, 16)), -0.2, 0.2), 0.0, 4.0),
    }


def reference(data, send_list, footprint_slot, footprint, colour, correlation, correlation_gram, traces_init):
    owner_dev = (jnp.arange(K, dtype=jnp.int32) // K_DEV).astype(jnp.int32)
    source = (footprint_slot // CAP).astype(jnp.int32)
    slot_pos = (footprint_slot % CAP).astype(jnp.int32)
    local_block = send_list[source, owner_dev[:, None], slot_pos]
    block_id = (source * VB_DEV + local_block).astype(jnp.int32)
    weights32 = footprint.astype(jnp.float32)
    self_gram = lax.optimization_barrier(jnp.sum(weights32 * weights32, axis=(1, 2)))

    def project(inputs):
        block_rows, weight_rows = inputs
        picked = data[block_rows].astype(jnp.float32)
        return jnp.einsum('kjtv,kjv->tk', picked, weight_rows.astype(jnp.float32))
    batches = K // K_DEV
    pieces = lax.map(project, (block_id.reshape(batches, K_DEV, FPB), footprint.reshape(batches, K_DEV, FPB, VOX)))
    projected = jnp.transpose(pieces, (1, 0, 2)).reshape(FRAMES, K)
    traces = traces_init
    for step_colour in range(4):
        neighbour_sum = jnp.zeros((FRAMES, K), jnp.float32)
        for column in range(OV):
            neighbour_sum = neighbour_sum + correlation_gram[:, column][None, :] * traces[:, correlation[:, column]]
        fresh = jnp.maximum((projected - neighbour_sum) / self_gram[None, :], 0.0)
        traces = jnp.where((colour == step_colour)[None, :], fresh, traces)
    trace_rms = jnp.sqrt(lax.optimization_barrier(jnp.mean(traces * traces, axis=0)) + 1e-06)
    return (traces, trace_rms)
```

```python
import functools

import jax
import jax.numpy as jnp
from jax import lax
from jax.experimental import pallas as pl
from jax.experimental.pallas import tpu as pltpu
from jax.sharding import PartitionSpec as P

REACH = (
    (0, 0), (1, 0), (-1, 0), (0, 1),
    (1, 1), (-1, 1), (2, 0), (-2, 0),
    (3, 0), (-3, 0), (2, 1), (-2, 1),
)
NEAR = REACH[:4]
LANES = 128
QUARTER = 32
DATA_ROWS = 64
META_ROWS = 32
VMEM_LIMIT = 48 * 2 ** 20
NT = (((1,), (1,)), ((), ()))


def iota(shape, dim):
    return lax.broadcasted_iota(jnp.int32, shape, dim)


def reach_at(device, near):
    return REACH.index((device[0] + near[0], (device[1] + near[1]) % 2))


def tile_at(me, rel, n):
    return lax.rem(me + rel[0] + rel[1] * (n // 2) + n, n)


def dot(a, b):
    return jnp.dot(a, b, preferred_element_type=jnp.float32)


def dot_nt(a, b):
    return lax.dot_general(a, b, NT, preferred_element_type=jnp.float32)


def split2(x):
    hi = x.astype(jnp.bfloat16).astype(jnp.float32)
    return hi, x - hi


def split3(x):
    hi, rest = split2(x)
    mid, low = split2(rest)
    return jnp.concatenate([hi, mid, low], axis=0).astype(jnp.bfloat16)


def join3(y):
    rows = y.shape[0] // 3
    return y[:rows] + y[rows : 2 * rows] + y[2 * rows :]


def dot_split(x, b_hi, b_lo):
    hi, low = split2(x)
    rows = x.shape[0]
    both = dot(jnp.concatenate([hi, low], axis=0).astype(jnp.bfloat16), b_hi)
    return both[:rows] + both[rows:] + dot(hi.astype(jnp.bfloat16), b_lo)


def put_split(hi_ref, lo_ref, x, place=slice(None)):
    hi, low = split2(x)
    hi_ref[place, :] = hi.astype(jnp.bfloat16)
    lo_ref[place, :] = low.astype(jnp.bfloat16)


def places(colour_row):
    in_class = colour_row == iota((8, LANES), 0)
    before = (iota((LANES, LANES), 0) < iota((LANES, LANES), 1)).astype(jnp.bfloat16)
    counts = dot(in_class.astype(jnp.bfloat16), before)
    rank = jnp.sum(jnp.where(in_class, counts, 0.0), axis=0, keepdims=True)
    return rank + (colour_row * QUARTER).astype(jnp.float32)


def pack_kernel(n, send_ref, data_ref, colour_ref, corr_ref, gram_ref, init_ref, out_ref, own_ref):
    me = lax.axis_index("tile")
    lane = iota((8, LANES), 1)
    row = iota((8, LANES), 0)
    pos = places(colour_ref[...])
    order = (iota((LANES, LANES), 0).astype(jnp.float32) == pos).astype(jnp.bfloat16)
    ids = corr_ref[...]
    away = jnp.bitwise_and(lax.shift_right_logical(ids, 7) - me, n - 1)
    which = jnp.where(away == 0, 0, jnp.where(away == 1, 1, jnp.where(away == n - 1, 2, 3)))
    code = which * LANES + jnp.bitwise_and(ids, LANES - 1) - 2 * LANES
    gram_hi, gram_lo = split2(gram_ref[...])
    init_hi, init_lo = split2(init_ref[...])
    rows = [code.astype(jnp.float32), gram_hi, gram_lo, init_hi, init_lo, lane.astype(jnp.float32)]
    placed = dot_nt(jnp.concatenate(rows, axis=0).astype(jnp.bfloat16), order)
    code, gram_hi, gram_lo, init_hi, init_lo, ident = [placed[8 * i : 8 * i + 8] for i in range(6)]
    own_ref[0:8, :] = code
    own_ref[8:16, :] = gram_hi + gram_lo
    own_ref[16:24, :] = jnp.broadcast_to(pos, (8, LANES))
    first = jnp.where(lane < 64, pltpu.roll(code, 96, 1), pltpu.roll(gram_hi, 32, 1))
    named = jnp.where(row == 0, pltpu.roll(ident, 64, 1), ident)
    second = jnp.where(lane < 64, pltpu.roll(gram_lo, 96, 1), named)
    meta = jnp.concatenate([first, second, init_hi, init_lo], axis=0).astype(jnp.bfloat16)
    for target in range(n):
        out_ref[target, DATA_ROWS:, :] = meta
        blocks = [data_ref[send_ref[c, target]].astype(jnp.float32) for c in range(8)]
        out_ref[target, :DATA_ROWS, :] = jnp.concatenate(blocks, axis=0).astype(jnp.bfloat16)


def names_column(meta):
    lane = iota((1, LANES), 1)
    named = jnp.where(lane < 64, pltpu.roll(meta[8:9], 64, 1), meta[9:10])
    eye = iota((LANES, LANES), 0) == iota((LANES, LANES), 1)
    spread = jnp.where(eye, named, 0.0).astype(jnp.bfloat16)
    return dot(spread, jnp.ones((LANES, LANES), jnp.bfloat16))


def listed(names, codes, weights):
    total = None
    for i in range(codes.shape[0]):
        term = jnp.where(names == codes[i : i + 1], weights[i : i + 1], 0.0)
        total = term if total is None else total + term
    return total


def project_kernel(n, tm, recv_ref, fp_ref, slot_ref, own_ref, out_ref, sg_ref, a3h_ref, a3l_ref):
    me = lax.axis_index("tile")
    lane = iota((8, LANES), 1)
    row = iota((8, LANES), 0)
    wide = 8 * LANES
    widen = (lax.shift_right_logical(iota((LANES, wide), 1), 3) == iota((LANES, wide), 0)).astype(jnp.bfloat16)
    narrow = jnp.concatenate([slot_ref[...].astype(jnp.float32), own_ref[16:24, :]], axis=0)
    if n * 8 <= 256:
        wider = dot(narrow.astype(jnp.bfloat16), widen)
    else:
        wider = join3(dot(split3(narrow), widen))
    mine = jnp.bitwise_and(iota((8, wide), 1), 7) == iota((8, wide), 0)
    slot_row = jnp.sum(jnp.where(mine, wider[0:8], 0.0), axis=0, keepdims=True)
    slot_row = jnp.broadcast_to(slot_row, (8, wide))
    order = (iota((LANES, wide), 0).astype(jnp.float32) == wider[8:9]).astype(jnp.bfloat16)
    weights = fp_ref[...]
    total = jnp.zeros((8, wide), jnp.float32)
    group = 4
    for source in range(0, n, group):
        blocks = recv_ref[source : source + group, :DATA_ROWS, :].reshape(group * DATA_ROWS, LANES)
        product = dot_nt(blocks, weights)
        for c in range(group * 8):
            hit = slot_row == float(source * 8 + c)
            total = total + jnp.where(hit, product[8 * c : 8 * c + 8], 0.0)
    wide32 = weights.astype(jnp.float32)
    square_hi, square_lo = split2(wide32 * wide32)
    ones = jnp.ones((8, LANES), jnp.bfloat16)
    squares = dot_nt(ones, square_hi.astype(jnp.bfloat16)) + dot_nt(ones, square_lo.astype(jnp.bfloat16))
    placed = join3(dot_nt(split3(jnp.concatenate([total, squares], axis=0)), order))
    projected, gram = placed[0:8], placed[8:16]
    sg_ref[...] = gram
    codes, grams = own_ref[0:8, :], own_ref[8:16, :]
    after = lax.shift_right_logical(iota((LANES, LANES), 0), 5) > lax.shift_right_logical(iota((LANES, LANES), 1), 5)
    coefs, starts = [], []
    for r, rel in enumerate(NEAR):
        meta = recv_ref[tile_at(me, rel, n), DATA_ROWS:, :].astype(jnp.float32)
        names = names_column(meta) + float(r * LANES - 2 * LANES)
        coefs.append(listed(names, codes, grams))
        starts.append(meta[16:24] + meta[24:32])
    late = jnp.concatenate([jnp.where(after, coef, 0.0) for coef in coefs], axis=0)
    late_hi, late_lo = split2(late)
    held = dot_split(
        jnp.concatenate(starts, axis=1), late_hi.astype(jnp.bfloat16), late_lo.astype(jnp.bfloat16)
    )
    for c in range(3):
        for p in range(4):
            source = coefs[(p - c) % 4][c * QUARTER : (c + 1) * QUARTER]
            start = c * LANES + p * QUARTER
            put_split(a3h_ref, a3l_ref, source, slice(start, start + QUARTER))
    base = projected - held
    message = jnp.where(lane < QUARTER, jnp.maximum(base / gram, 0.0), base)
    grams12 = jnp.where(row == 0, pltpu.roll(gram, 64, 1), pltpu.roll(gram, 32, 1))
    others = jnp.where(lane < 96, message, grams12)
    for t in range(n * tm):
        out_ref[t] = others
    for i, rel in enumerate(REACH):
        source = message if i == 0 else others
        turned = source if i % 4 == 0 else pltpu.roll(source, QUARTER * (i % 4), 1)
        target = tile_at(me, (-rel[0], rel[1]), n)
        for t in range(tm):
            out_ref[target * tm + t] = turned


def coef_kernel(n, recv_ref, a1h_ref, a1l_ref, a2h_ref, a2l_ref):
    me = lax.axis_index("tile")
    block = lax.shift_right_logical(iota((8, LANES), 1), 5)
    names, codes, gram_hi, gram_lo = [], [], [], []
    for i, rel in enumerate(REACH):
        meta = recv_ref[tile_at(me, rel, n), DATA_ROWS:, :].astype(jnp.float32)
        names.append(names_column(meta) + float(i * LANES))
        if i < 8:
            code = meta[0:8].astype(jnp.int32) + 2 * LANES
            which = lax.shift_right_logical(code, 7)
            at = [reach_at(rel, near) for near in NEAR]
            place = jnp.where(
                which == 0, at[0], jnp.where(which == 1, at[1], jnp.where(which == 2, at[2], at[3]))
            )
            code = place * LANES + jnp.bitwise_and(code, LANES - 1)
            codes.append(code.astype(jnp.float32))
            gram_hi.append(meta[0:8])
            gram_lo.append(meta[8:16])

    def gathered(parts, group, colour, start):
        out = None
        for q in range(4):
            p = (q + colour) % 4
            shift = (QUARTER * p - start) % LANES
            turned = parts[4 * group + q]
            turned = turned if shift == 0 else pltpu.roll(turned, shift, 1)
            out = turned if out is None else jnp.where(block == p, turned, out)
        return out

    first = jnp.concatenate([name[0:QUARTER] for name in names], axis=0)
    for group in range(2):
        code = gathered(codes, group, 1, 0)
        gram = gathered(gram_hi, group, 1, 64) + gathered(gram_lo, group, 1, 0)
        hi, low = split2(listed(first, code, gram))
        a1h_ref[:, group * LANES : (group + 1) * LANES] = hi.astype(jnp.bfloat16)
        a1l_ref[:, group * LANES : (group + 1) * LANES] = low.astype(jnp.bfloat16)
    earlier = [name[0:QUARTER] for name in names[:8]]
    for group in range(2):
        earlier += [names[4 * group + (p - 1) % 4][QUARTER : 2 * QUARTER] for p in range(4)]
    code = gathered(codes, 0, 2, 32)
    gram = gathered(gram_hi, 0, 2, 96) + gathered(gram_lo, 0, 2, 32)
    put_split(a2h_ref, a2l_ref, listed(jnp.concatenate(earlier, axis=0), code, gram))


def sweep_kernel(
    n, tm, recv_ref, sg_ref, own_ref, a1h_ref, a1l_ref, a2h_ref, a2l_ref, a3h_ref, a3l_ref, traces_ref, rms_ref
):
    me = lax.axis_index("tile")
    frames = 8 * tm
    block = lax.shift_right_logical(iota((frames, LANES), 1), 5)
    messages = []
    for rel in REACH:
        first = tile_at(me, rel, n) * tm
        messages.append(jnp.concatenate([recv_ref[first + t] for t in range(tm)], axis=0))

    def gathered(group, turn):
        out = messages[4 * group]
        for q in range(4):
            if q or turn:
                out = jnp.where(block == (q + turn) % 4, messages[4 * group + q], out)
        return out

    gram = sg_ref[0:1, :]
    first_lane = iota((1, LANES), 1)

    def gram_of(group, colour):
        rows = gathered(group, 3)[colour - 1 : colour]
        rows = pltpu.roll(rows, 64 if colour == 1 else 96, 1)
        if group:
            return rows
        own = lax.shift_right_logical(first_lane, 5) == colour
        return jnp.where(own, gram, rows)

    x0 = [gathered(group, 0) for group in range(3)]
    n1 = dot_split(jnp.concatenate(x0, axis=1), a1h_ref[...], a1l_ref[...])
    x1 = [
        jnp.maximum((gathered(g, 1) - n1[:, g * LANES : (g + 1) * LANES]) / gram_of(g, 1), 0.0) for g in range(2)
    ]
    n2 = dot_split(jnp.concatenate([x0[0], x0[1], x1[0], x1[1]], axis=1), a2h_ref[...], a2l_ref[...])
    x2 = jnp.maximum((gathered(0, 2) - n2) / gram_of(0, 2), 0.0)
    n3 = dot_split(jnp.concatenate([x0[0], x1[0], x2], axis=1), a3h_ref[...], a3l_ref[...])
    x3 = jnp.maximum((messages[0] - n3) / gram, 0.0)
    own = jnp.where(
        block == 0, messages[0], jnp.where(block == 1, x1[0], jnp.where(block == 2, x2, x3))
    )
    energy = jnp.sum(own * own, axis=0, keepdims=True)
    half = lax.axis_index("tm")
    mine = own[0:8]
    for t in range(1, tm):
        mine = jnp.where(half == t, own[8 * t : 8 * t + 8], mine)
    order = (iota((LANES, LANES), 0).astype(jnp.float32) == own_ref[16:17, :]).astype(jnp.bfloat16)
    stacked = jnp.concatenate([mine, jnp.broadcast_to(energy, (8, LANES))], axis=0)
    placed = join3(dot(split3(stacked), order))
    traces_ref[...] = placed[0:8]
    rms_ref[...] = jnp.sqrt(placed[8:9] / frames + 1e-06)


def shards(
    data, send_list, footprint_slot, footprint, colour, correlation, correlation_gram, traces_init
):
    n = lax.axis_size("tile")
    tm = lax.axis_size("tm")
    f32, bf16 = jnp.float32, jnp.bfloat16
    shape = jax.ShapeDtypeStruct
    params = pltpu.CompilerParams(vmem_limit_bytes=VMEM_LIMIT)
    vmem = pl.BlockSpec(memory_space=pltpu.VMEM)
    smem = pl.BlockSpec(memory_space=pltpu.SMEM)

    def call(body, outs, ins):
        return pl.pallas_call(
            body, out_shape=outs, in_specs=ins, out_specs=[vmem] * len(outs), compiler_params=params
        )

    outgoing, own = call(
        functools.partial(pack_kernel, n),
        [shape((n, DATA_ROWS + META_ROWS, LANES), bf16), shape((24, LANES), f32)],
        [smem] + [vmem] * 5,
    )(send_list[0].T, data, colour.reshape(1, LANES), correlation.T, correlation_gram.T, traces_init)
    arrived = lax.all_to_all(outgoing, "tile", split_axis=0, concat_axis=0, tiled=True)
    message, self_gram, a3h, a3l = call(
        functools.partial(project_kernel, n, tm),
        [shape((n * tm, 8, LANES), f32), shape((8, LANES), f32)] + [shape((384, LANES), bf16)] * 2,
        [vmem] * 4,
    )(arrived, footprint.reshape(8 * LANES, LANES), footprint_slot.T, own)
    messages = lax.all_to_all(message, ("tile", "tm"), split_axis=0, concat_axis=0, tiled=True)
    a1h, a1l, a2h, a2l = call(
        functools.partial(coef_kernel, n),
        [shape((384, 2 * LANES), bf16)] * 2 + [shape((512, LANES), bf16)] * 2,
        [vmem],
    )(arrived)
    traces, rms = call(
        functools.partial(sweep_kernel, n, tm),
        [shape((8, LANES), f32), shape((1, LANES), f32)],
        [vmem] * 9,
    )(messages, self_gram, own, a1h, a1l, a2h, a2l, a3h, a3l)
    return (traces, rms.reshape(LANES))


def solution(mesh):
    placed = (
        P("tile", "tm", None),
        P("tile", None, None),
        P("tile", None),
        P("tile", None, None),
        P("tile"),
        P("tile", None),
        P("tile", None),
        P("tm", "tile"),
    )
    return jax.shard_map(
        shards, mesh=mesh, in_specs=placed, out_specs=(P("tm", "tile"), P("tile")), check_vma=False
    )
```

```python
import functools

import jax
import jax.numpy as jnp
from jax import lax
from jax.experimental import pallas as pl
from jax.experimental.pallas import tpu as pltpu
from jax.sharding import PartitionSpec as P

REACH = (
    (0, 0), (1, 0), (-1, 0), (0, 1),
    (1, 1), (-1, 1), (2, 0), (-2, 0),
    (3, 0), (-3, 0), (2, 1), (-2, 1),
)
NEAR = REACH[:4]
LANES = 128
QUARTER = 32
DATA_ROWS = 64
META_ROWS = 32
VMEM_LIMIT = 48 * 2 ** 20
PACK_LIMIT = 60 * 10 ** 6
NT = (((1,), (1,)), ((), ()))


def iota(shape, dim):
    return lax.broadcasted_iota(jnp.int32, shape, dim)


def reach_at(device, near):
    return REACH.index((device[0] + near[0], (device[1] + near[1]) % 2))


def tile_at(me, rel, n):
    return lax.rem(me + rel[0] + rel[1] * (n // 2) + n, n)


def dot(a, b):
    return jnp.dot(a, b, preferred_element_type=jnp.float32)


def dot_nt(a, b):
    return lax.dot_general(a, b, NT, preferred_element_type=jnp.float32)


def split2(x):
    hi = x.astype(jnp.bfloat16).astype(jnp.float32)
    return hi, x - hi


def split3(x):
    hi, rest = split2(x)
    mid, low = split2(rest)
    return jnp.concatenate([hi, mid, low], axis=0).astype(jnp.bfloat16)


def join3(y):
    rows = y.shape[0] // 3
    return y[:rows] + y[rows : 2 * rows] + y[2 * rows :]


def dot_split(x, b_hi, b_lo):
    hi, low = split2(x)
    rows = x.shape[0]
    both = dot(jnp.concatenate([hi, low], axis=0).astype(jnp.bfloat16), b_hi)
    return both[:rows] + both[rows:] + dot(hi.astype(jnp.bfloat16), b_lo)


def put_split(hi_ref, lo_ref, x, place=slice(None)):
    hi, low = split2(x)
    hi_ref[place, :] = hi.astype(jnp.bfloat16)
    lo_ref[place, :] = low.astype(jnp.bfloat16)


def places(colour_row):
    in_class = colour_row == iota((8, LANES), 0)
    before = (iota((LANES, LANES), 0) < iota((LANES, LANES), 1)).astype(jnp.bfloat16)
    counts = dot(in_class.astype(jnp.bfloat16), before)
    rank = jnp.sum(jnp.where(in_class, counts, 0.0), axis=0, keepdims=True)
    return rank + (colour_row * QUARTER).astype(jnp.float32)


def pack_kernel(n, *refs):
    sources, (out_ref, own_ref), held, sems = refs[:7], refs[7:9], refs[9:16], refs[16]
    send_ref, data_ref, colour_ref, corr_ref, gram_ref, init_ref, slot_ref = held
    copies = [pltpu.make_async_copy(a, b, sems.at[i]) for i, (a, b) in enumerate(zip(sources, held))]
    for copy in copies:
        copy.start()
    me = lax.axis_index("tile")
    lane = iota((8, LANES), 1)
    row = iota((8, LANES), 0)
    for copy in copies[2:]:
        copy.wait()
    own_ref[24:32, :] = slot_ref[...].astype(jnp.float32)
    pos = places(colour_ref[...])
    order = (iota((LANES, LANES), 0).astype(jnp.float32) == pos).astype(jnp.bfloat16)
    ids = corr_ref[...]
    away = jnp.bitwise_and(lax.shift_right_logical(ids, 7) - me, n - 1)
    which = jnp.where(away == 0, 0, jnp.where(away == 1, 1, jnp.where(away == n - 1, 2, 3)))
    code = which * LANES + jnp.bitwise_and(ids, LANES - 1) - 2 * LANES
    gram_hi, gram_lo = split2(gram_ref[...])
    init_hi, init_lo = split2(init_ref[...])
    rows = [code.astype(jnp.float32), gram_hi, gram_lo, init_hi, init_lo, lane.astype(jnp.float32)]
    placed = dot_nt(jnp.concatenate(rows, axis=0).astype(jnp.bfloat16), order)
    code, gram_hi, gram_lo, init_hi, init_lo, ident = [placed[8 * i : 8 * i + 8] for i in range(6)]
    own_ref[0:8, :] = code
    own_ref[8:16, :] = gram_hi + gram_lo
    own_ref[16:24, :] = jnp.broadcast_to(pos, (8, LANES))
    first = jnp.where(lane < 64, pltpu.roll(code, 96, 1), pltpu.roll(gram_hi, 32, 1))
    named = jnp.where(row == 0, pltpu.roll(ident, 64, 1), ident)
    second = jnp.where(lane < 64, pltpu.roll(gram_lo, 96, 1), named)
    meta = jnp.concatenate([first, second, init_hi, init_lo], axis=0).astype(jnp.bfloat16)
    for copy in copies[:2]:
        copy.wait()
    for target in range(n):
        out_ref[target, DATA_ROWS:, :] = meta
        blocks = [data_ref[send_ref[c, target]].astype(jnp.float32) for c in range(8)]
        out_ref[target, :DATA_ROWS, :] = jnp.concatenate(blocks, axis=0).astype(jnp.bfloat16)


def names_column(meta):
    lane = iota((1, LANES), 1)
    named = jnp.where(lane < 64, pltpu.roll(meta[8:9], 64, 1), meta[9:10])
    eye = iota((LANES, LANES), 0) == iota((LANES, LANES), 1)
    spread = jnp.where(eye, named, 0.0).astype(jnp.bfloat16)
    return dot(spread, jnp.ones((LANES, LANES), jnp.bfloat16))


def listed(names, codes, weights):
    total = None
    for i in range(codes.shape[0]):
        term = jnp.where(names == codes[i : i + 1], weights[i : i + 1], 0.0)
        total = term if total is None else total + term
    return total


def project_kernel(n, tm, recv_ref, fp_ref, own_ref, out_ref, sg_ref, a3h_ref, a3l_ref):
    me = lax.axis_index("tile")
    lane = iota((8, LANES), 1)
    row = iota((8, LANES), 0)
    wide = 8 * LANES
    widen = (lax.shift_right_logical(iota((LANES, wide), 1), 3) == iota((LANES, wide), 0)).astype(jnp.bfloat16)
    narrow = own_ref[16:32, :]
    if n * 8 <= 256:
        wider = dot(narrow.astype(jnp.bfloat16), widen)
    else:
        wider = join3(dot(split3(narrow), widen))
    mine = jnp.bitwise_and(iota((8, wide), 1), 7) == iota((8, wide), 0)
    slot_row = jnp.sum(jnp.where(mine, wider[8:16], 0.0), axis=0, keepdims=True)
    slot_row = jnp.broadcast_to(slot_row, (8, wide))
    order = (iota((LANES, wide), 0).astype(jnp.float32) == wider[0:1]).astype(jnp.bfloat16)
    weights = fp_ref[...]
    total = jnp.zeros((8, wide), jnp.float32)
    group = 4
    for source in range(0, n, group):
        blocks = recv_ref[source : source + group, :DATA_ROWS, :].reshape(group * DATA_ROWS, LANES)
        product = dot_nt(blocks, weights)
        for c in range(group * 8):
            hit = slot_row == float(source * 8 + c)
            total = total + jnp.where(hit, product[8 * c : 8 * c + 8], 0.0)
    wide32 = weights.astype(jnp.float32)
    square_hi, square_lo = split2(wide32 * wide32)
    ones = jnp.ones((8, LANES), jnp.bfloat16)
    squares = dot_nt(ones, square_hi.astype(jnp.bfloat16)) + dot_nt(ones, square_lo.astype(jnp.bfloat16))
    placed = join3(dot_nt(split3(jnp.concatenate([total, squares], axis=0)), order))
    projected, gram = placed[0:8], placed[8:16]
    sg_ref[...] = gram
    codes, grams = own_ref[0:8, :], own_ref[8:16, :]
    after = lax.shift_right_logical(iota((LANES, LANES), 0), 5) > lax.shift_right_logical(iota((LANES, LANES), 1), 5)
    coefs, starts = [], []
    for r, rel in enumerate(NEAR):
        meta = recv_ref[tile_at(me, rel, n), DATA_ROWS:, :].astype(jnp.float32)
        names = names_column(meta) + float(r * LANES - 2 * LANES)
        coefs.append(listed(names, codes, grams))
        starts.append(meta[16:24] + meta[24:32])
    late = jnp.concatenate([jnp.where(after, coef, 0.0) for coef in coefs], axis=0)
    late_hi, late_lo = split2(late)
    held = dot_split(
        jnp.concatenate(starts, axis=1), late_hi.astype(jnp.bfloat16), late_lo.astype(jnp.bfloat16)
    )
    for c in range(3):
        for p in range(4):
            source = coefs[(p - c) % 4][c * QUARTER : (c + 1) * QUARTER]
            start = c * LANES + p * QUARTER
            put_split(a3h_ref, a3l_ref, source, slice(start, start + QUARTER))
    base = projected - held
    message = jnp.where(lane < QUARTER, jnp.maximum(base / gram, 0.0), base)
    grams12 = jnp.where(row == 0, pltpu.roll(gram, 64, 1), pltpu.roll(gram, 32, 1))
    others = jnp.where(lane < 96, message, grams12)
    for t in range(n * tm):
        out_ref[t] = others
    for i, rel in enumerate(REACH):
        source = message if i == 0 else others
        turned = source if i % 4 == 0 else pltpu.roll(source, QUARTER * (i % 4), 1)
        target = tile_at(me, (-rel[0], rel[1]), n)
        for t in range(tm):
            out_ref[target * tm + t] = turned


def coef_kernel(n, recv_ref, a1h_ref, a1l_ref, a2h_ref, a2l_ref):
    me = lax.axis_index("tile")
    block = lax.shift_right_logical(iota((8, LANES), 1), 5)
    names, codes, gram_hi, gram_lo = [], [], [], []
    for i, rel in enumerate(REACH):
        meta = recv_ref[tile_at(me, rel, n), DATA_ROWS:, :].astype(jnp.float32)
        names.append(names_column(meta) + float(i * LANES))
        if i < 8:
            code = meta[0:8].astype(jnp.int32) + 2 * LANES
            which = lax.shift_right_logical(code, 7)
            at = [reach_at(rel, near) for near in NEAR]
            place = jnp.where(
                which == 0, at[0], jnp.where(which == 1, at[1], jnp.where(which == 2, at[2], at[3]))
            )
            code = place * LANES + jnp.bitwise_and(code, LANES - 1)
            codes.append(code.astype(jnp.float32))
            gram_hi.append(meta[0:8])
            gram_lo.append(meta[8:16])

    def gathered(parts, group, colour, start):
        out = None
        for q in range(4):
            p = (q + colour) % 4
            shift = (QUARTER * p - start) % LANES
            turned = parts[4 * group + q]
            turned = turned if shift == 0 else pltpu.roll(turned, shift, 1)
            out = turned if out is None else jnp.where(block == p, turned, out)
        return out

    first = jnp.concatenate([name[0:QUARTER] for name in names], axis=0)
    for group in range(2):
        code = gathered(codes, group, 1, 0)
        gram = gathered(gram_hi, group, 1, 64) + gathered(gram_lo, group, 1, 0)
        hi, low = split2(listed(first, code, gram))
        a1h_ref[:, group * LANES : (group + 1) * LANES] = hi.astype(jnp.bfloat16)
        a1l_ref[:, group * LANES : (group + 1) * LANES] = low.astype(jnp.bfloat16)
    earlier = [name[0:QUARTER] for name in names[:8]]
    for group in range(2):
        earlier += [names[4 * group + (p - 1) % 4][QUARTER : 2 * QUARTER] for p in range(4)]
    code = gathered(codes, 0, 2, 32)
    gram = gathered(gram_hi, 0, 2, 96) + gathered(gram_lo, 0, 2, 32)
    put_split(a2h_ref, a2l_ref, listed(jnp.concatenate(earlier, axis=0), code, gram))


def sweep_kernel(
    n, tm, recv_ref, sg_ref, own_ref, a1h_ref, a1l_ref, a2h_ref, a2l_ref, a3h_ref, a3l_ref, traces_ref, rms_ref
):
    me = lax.axis_index("tile")
    frames = 8 * tm
    block = lax.shift_right_logical(iota((frames, LANES), 1), 5)
    messages = []
    for rel in REACH:
        first = tile_at(me, rel, n) * tm
        messages.append(jnp.concatenate([recv_ref[first + t] for t in range(tm)], axis=0))

    def gathered(group, turn):
        out = messages[4 * group]
        for q in range(4):
            if q or turn:
                out = jnp.where(block == (q + turn) % 4, messages[4 * group + q], out)
        return out

    gram = sg_ref[0:1, :]
    first_lane = iota((1, LANES), 1)

    def gram_of(group, colour):
        rows = gathered(group, 3)[colour - 1 : colour]
        rows = pltpu.roll(rows, 64 if colour == 1 else 96, 1)
        if group:
            return rows
        own = lax.shift_right_logical(first_lane, 5) == colour
        return jnp.where(own, gram, rows)

    x0 = [gathered(group, 0) for group in range(3)]
    n1 = dot_split(jnp.concatenate(x0, axis=1), a1h_ref[...], a1l_ref[...])
    x1 = [
        jnp.maximum((gathered(g, 1) - n1[:, g * LANES : (g + 1) * LANES]) / gram_of(g, 1), 0.0) for g in range(2)
    ]
    n2 = dot_split(jnp.concatenate([x0[0], x0[1], x1[0], x1[1]], axis=1), a2h_ref[...], a2l_ref[...])
    x2 = jnp.maximum((gathered(0, 2) - n2) / gram_of(0, 2), 0.0)
    n3 = dot_split(jnp.concatenate([x0[0], x1[0], x2], axis=1), a3h_ref[...], a3l_ref[...])
    x3 = jnp.maximum((messages[0] - n3) / gram, 0.0)
    own = jnp.where(
        block == 0, messages[0], jnp.where(block == 1, x1[0], jnp.where(block == 2, x2, x3))
    )
    energy = jnp.sum(own * own, axis=0, keepdims=True)
    half = lax.axis_index("tm")
    mine = own[0:8]
    for t in range(1, tm):
        mine = jnp.where(half == t, own[8 * t : 8 * t + 8], mine)
    order = (iota((LANES, LANES), 0).astype(jnp.float32) == own_ref[16:17, :]).astype(jnp.bfloat16)
    stacked = jnp.concatenate([mine, jnp.broadcast_to(energy, (8, LANES))], axis=0)
    placed = join3(dot(split3(stacked), order))
    traces_ref[...] = placed[0:8]
    rms_ref[...] = jnp.sqrt(placed[8:9] / frames + 1e-06)


def shards(
    data, send_list, footprint_slot, footprint, colour, correlation, correlation_gram, traces_init
):
    n = lax.axis_size("tile")
    tm = lax.axis_size("tm")
    f32, bf16 = jnp.float32, jnp.bfloat16
    shape = jax.ShapeDtypeStruct
    vmem = pl.BlockSpec(memory_space=pltpu.VMEM)
    hbm = pl.BlockSpec(memory_space=pltpu.HBM)

    def call(body, outs, ins, scratch=(), limit=VMEM_LIMIT):
        return pl.pallas_call(
            body,
            out_shape=outs,
            in_specs=ins,
            out_specs=[vmem] * len(outs),
            scratch_shapes=scratch,
            compiler_params=pltpu.CompilerParams(vmem_limit_bytes=limit),
        )

    inputs = (
        send_list[0].T, data, colour.reshape(1, LANES), correlation.T, correlation_gram.T, traces_init,
        footprint_slot.T,
    )
    outgoing, own = call(
        functools.partial(pack_kernel, n),
        [shape((n, DATA_ROWS + META_ROWS, LANES), bf16), shape((32, LANES), f32)],
        [hbm] * 7,
        [pltpu.SMEM(inputs[0].shape, jnp.int32)]
        + [pltpu.VMEM(x.shape, x.dtype) for x in inputs[1:]]
        + [pltpu.SemaphoreType.DMA((7,))],
        PACK_LIMIT,
    )(*inputs)
    arrived = lax.all_to_all(outgoing, "tile", split_axis=0, concat_axis=0, tiled=True)
    message, self_gram, a3h, a3l = call(
        functools.partial(project_kernel, n, tm),
        [shape((n * tm, 8, LANES), f32), shape((8, LANES), f32)] + [shape((384, LANES), bf16)] * 2,
        [vmem] * 3,
    )(arrived, footprint.reshape(8 * LANES, LANES), own)
    messages = lax.all_to_all(message, ("tile", "tm"), split_axis=0, concat_axis=0, tiled=True)
    a1h, a1l, a2h, a2l = call(
        functools.partial(coef_kernel, n),
        [shape((384, 2 * LANES), bf16)] * 2 + [shape((512, LANES), bf16)] * 2,
        [vmem],
    )(arrived)
    traces, rms = call(
        functools.partial(sweep_kernel, n, tm),
        [shape((8, LANES), f32), shape((1, LANES), f32)],
        [vmem] * 9,
    )(messages, self_gram, own, a1h, a1l, a2h, a2l, a3h, a3l)
    return (traces, rms.reshape(LANES))


def solution(mesh):
    placed = (
        P("tile", "tm", None),
        P("tile", None, None),
        P("tile", None),
        P("tile", None, None),
        P("tile"),
        P("tile", None),
        P("tile", None),
        P("tm", "tile"),
    )
    return jax.shard_map(
        shards, mesh=mesh, in_specs=placed, out_specs=(P("tm", "tile"), P("tile")), check_vma=False
    )
```

```python
import functools

import jax
import jax.numpy as jnp
from jax import lax
from jax.experimental import pallas as pl
from jax.experimental.pallas import tpu as pltpu
from jax.sharding import PartitionSpec as P

REACH = (
    (0, 0), (1, 0), (-1, 0), (0, 1),
    (1, 1), (-1, 1), (2, 0), (-2, 0),
    (3, 0), (-3, 0), (2, 1), (-2, 1),
)
NEAR = REACH[:4]
LANES = 128
QUARTER = 32
DATA_ROWS = 64
META_ROWS = 32
VMEM_LIMIT = 48 * 2 ** 20
PACK_LIMIT = 48 * 2 ** 20
NT = (((1,), (1,)), ((), ()))


def iota(shape, dim):
    return lax.broadcasted_iota(jnp.int32, shape, dim)


def reach_at(device, near):
    return REACH.index((device[0] + near[0], (device[1] + near[1]) % 2))


def tile_at(me, rel, n):
    return lax.rem(me + rel[0] + rel[1] * (n // 2) + n, n)


def dot(a, b):
    return jnp.dot(a, b, preferred_element_type=jnp.float32)


def dot_nt(a, b):
    return lax.dot_general(a, b, NT, preferred_element_type=jnp.float32)


def split2(x):
    hi = x.astype(jnp.bfloat16).astype(jnp.float32)
    return hi, x - hi


def split3(x):
    hi, rest = split2(x)
    mid, low = split2(rest)
    return jnp.concatenate([hi, mid, low], axis=0).astype(jnp.bfloat16)


def join3(y):
    rows = y.shape[0] // 3
    return y[:rows] + y[rows : 2 * rows] + y[2 * rows :]


def dot_split(x, b_hi, b_lo):
    hi, low = split2(x)
    rows = x.shape[0]
    both = dot(jnp.concatenate([hi, low], axis=0).astype(jnp.bfloat16), b_hi)
    return both[:rows] + both[rows:] + dot(hi.astype(jnp.bfloat16), b_lo)


def put_split(hi_ref, lo_ref, x, place=slice(None)):
    hi, low = split2(x)
    hi_ref[place, :] = hi.astype(jnp.bfloat16)
    lo_ref[place, :] = low.astype(jnp.bfloat16)


def places(colour_row):
    in_class = colour_row == iota((8, LANES), 0)
    before = (iota((LANES, LANES), 0) < iota((LANES, LANES), 1)).astype(jnp.bfloat16)
    counts = dot(in_class.astype(jnp.bfloat16), before)
    rank = jnp.sum(jnp.where(in_class, counts, 0.0), axis=0, keepdims=True)
    return rank + (colour_row * QUARTER).astype(jnp.float32)


def pack_kernel(n, *refs):
    sources, (out_ref, own_ref), held, sems = refs[:7], refs[7:9], refs[9:16], refs[16]
    send_ref, data_ref, colour_ref, corr_ref, gram_ref, init_ref, slot_ref = held
    copies = [pltpu.make_async_copy(a, b, sems.at[i]) for i, (a, b) in enumerate(zip(sources, held))]
    for copy in copies:
        copy.start()
    me = lax.axis_index("tile")
    lane = iota((8, LANES), 1)
    row = iota((8, LANES), 0)
    for copy in copies[2:]:
        copy.wait()
    own_ref[24:32, :] = slot_ref[...].astype(jnp.float32)
    pos = places(colour_ref[...])
    order = (iota((LANES, LANES), 0).astype(jnp.float32) == pos).astype(jnp.bfloat16)
    ids = corr_ref[...]
    away = jnp.bitwise_and(lax.shift_right_logical(ids, 7) - me, n - 1)
    which = jnp.where(away == 0, 0, jnp.where(away == 1, 1, jnp.where(away == n - 1, 2, 3)))
    code = which * LANES + jnp.bitwise_and(ids, LANES - 1) - 2 * LANES
    gram_hi, gram_lo = split2(gram_ref[...])
    init_hi, init_lo = split2(init_ref[...])
    rows = [code.astype(jnp.float32), gram_hi, gram_lo, init_hi, init_lo, lane.astype(jnp.float32)]
    placed = dot_nt(jnp.concatenate(rows, axis=0).astype(jnp.bfloat16), order)
    code, gram_hi, gram_lo, init_hi, init_lo, ident = [placed[8 * i : 8 * i + 8] for i in range(6)]
    own_ref[0:8, :] = code
    own_ref[8:16, :] = gram_hi + gram_lo
    own_ref[16:24, :] = jnp.broadcast_to(pos, (8, LANES))
    first = jnp.where(lane < 64, pltpu.roll(code, 96, 1), pltpu.roll(gram_hi, 32, 1))
    named = jnp.where(row == 0, pltpu.roll(ident, 64, 1), ident)
    second = jnp.where(lane < 64, pltpu.roll(gram_lo, 96, 1), named)
    meta = jnp.concatenate([first, second, init_hi, init_lo], axis=0).astype(jnp.bfloat16)
    for copy in copies[:2]:
        copy.wait()
    for target in range(n):
        out_ref[target, DATA_ROWS:, :] = meta
        blocks = [data_ref[send_ref[c, target]].astype(jnp.float32) for c in range(8)]
        out_ref[target, :DATA_ROWS, :] = jnp.concatenate(blocks, axis=0).astype(jnp.bfloat16)


def names_column(meta):
    lane = iota((1, LANES), 1)
    named = jnp.where(lane < 64, pltpu.roll(meta[8:9], 64, 1), meta[9:10])
    eye = iota((LANES, LANES), 0) == iota((LANES, LANES), 1)
    spread = jnp.where(eye, named, 0.0).astype(jnp.bfloat16)
    return dot(spread, jnp.ones((LANES, LANES), jnp.bfloat16))


def listed(names, codes, weights):
    total = None
    for i in range(codes.shape[0]):
        term = jnp.where(names == codes[i : i + 1], weights[i : i + 1], 0.0)
        total = term if total is None else total + term
    return total


def project_kernel(n, tm, recv_ref, fp_ref, own_ref, out_ref, sg_ref, a3h_ref, a3l_ref):
    me = lax.axis_index("tile")
    lane = iota((8, LANES), 1)
    row = iota((8, LANES), 0)
    wide = 8 * LANES
    widen = (lax.shift_right_logical(iota((LANES, wide), 1), 3) == iota((LANES, wide), 0)).astype(jnp.bfloat16)
    narrow = own_ref[16:32, :]
    if n * 8 <= 256:
        wider = dot(narrow.astype(jnp.bfloat16), widen)
    else:
        wider = join3(dot(split3(narrow), widen))
    mine = jnp.bitwise_and(iota((8, wide), 1), 7) == iota((8, wide), 0)
    slot_row = jnp.sum(jnp.where(mine, wider[8:16], 0.0), axis=0, keepdims=True)
    slot_row = jnp.broadcast_to(slot_row, (8, wide))
    order = (iota((LANES, wide), 0).astype(jnp.float32) == wider[0:1]).astype(jnp.bfloat16)
    weights = fp_ref[...]
    total = jnp.zeros((8, wide), jnp.float32)
    group = 4
    for source in range(0, n, group):
        blocks = recv_ref[source : source + group, :DATA_ROWS, :].reshape(group * DATA_ROWS, LANES)
        product = dot_nt(blocks, weights)
        for c in range(group * 8):
            hit = slot_row == float(source * 8 + c)
            total = total + jnp.where(hit, product[8 * c : 8 * c + 8], 0.0)
    wide32 = weights.astype(jnp.float32)
    square_hi, square_lo = split2(wide32 * wide32)
    ones = jnp.ones((8, LANES), jnp.bfloat16)
    squares = dot_nt(ones, square_hi.astype(jnp.bfloat16)) + dot_nt(ones, square_lo.astype(jnp.bfloat16))
    placed = join3(dot_nt(split3(jnp.concatenate([total, squares], axis=0)), order))
    projected, gram = placed[0:8], placed[8:16]
    sg_ref[...] = gram
    codes, grams = own_ref[0:8, :], own_ref[8:16, :]
    after = lax.shift_right_logical(iota((LANES, LANES), 0), 5) > lax.shift_right_logical(iota((LANES, LANES), 1), 5)
    coefs, starts = [], []
    for r, rel in enumerate(NEAR):
        meta = recv_ref[tile_at(me, rel, n), DATA_ROWS:, :].astype(jnp.float32)
        names = names_column(meta) + float(r * LANES - 2 * LANES)
        coefs.append(listed(names, codes, grams))
        starts.append(meta[16:24] + meta[24:32])
    late = jnp.concatenate([jnp.where(after, coef, 0.0) for coef in coefs], axis=0)
    late_hi, late_lo = split2(late)
    held = dot_split(
        jnp.concatenate(starts, axis=1), late_hi.astype(jnp.bfloat16), late_lo.astype(jnp.bfloat16)
    )
    for c in range(3):
        for p in range(4):
            source = coefs[(p - c) % 4][c * QUARTER : (c + 1) * QUARTER]
            start = c * LANES + p * QUARTER
            put_split(a3h_ref, a3l_ref, source, slice(start, start + QUARTER))
    base = projected - held
    message = jnp.where(lane < QUARTER, jnp.maximum(base / gram, 0.0), base)
    grams12 = jnp.where(row == 0, pltpu.roll(gram, 64, 1), pltpu.roll(gram, 32, 1))
    others = jnp.where(lane < 96, message, grams12)
    for t in range(n * tm):
        out_ref[t] = others
    for i, rel in enumerate(REACH):
        source = message if i == 0 else others
        turned = source if i % 4 == 0 else pltpu.roll(source, QUARTER * (i % 4), 1)
        target = tile_at(me, (-rel[0], rel[1]), n)
        for t in range(tm):
            out_ref[target * tm + t] = turned


def coef_kernel(n, recv_ref, a1h_ref, a1l_ref, a2h_ref, a2l_ref):
    me = lax.axis_index("tile")
    block = lax.shift_right_logical(iota((8, LANES), 1), 5)
    names, codes, gram_hi, gram_lo = [], [], [], []
    for i, rel in enumerate(REACH):
        meta = recv_ref[tile_at(me, rel, n), DATA_ROWS:, :].astype(jnp.float32)
        names.append(names_column(meta) + float(i * LANES))
        if i < 8:
            code = meta[0:8].astype(jnp.int32) + 2 * LANES
            which = lax.shift_right_logical(code, 7)
            at = [reach_at(rel, near) for near in NEAR]
            place = jnp.where(
                which == 0, at[0], jnp.where(which == 1, at[1], jnp.where(which == 2, at[2], at[3]))
            )
            code = place * LANES + jnp.bitwise_and(code, LANES - 1)
            codes.append(code.astype(jnp.float32))
            gram_hi.append(meta[0:8])
            gram_lo.append(meta[8:16])

    def gathered(parts, group, colour, start):
        out = None
        for q in range(4):
            p = (q + colour) % 4
            shift = (QUARTER * p - start) % LANES
            turned = parts[4 * group + q]
            turned = turned if shift == 0 else pltpu.roll(turned, shift, 1)
            out = turned if out is None else jnp.where(block == p, turned, out)
        return out

    first = jnp.concatenate([name[0:QUARTER] for name in names], axis=0)
    for group in range(2):
        code = gathered(codes, group, 1, 0)
        gram = gathered(gram_hi, group, 1, 64) + gathered(gram_lo, group, 1, 0)
        hi, low = split2(listed(first, code, gram))
        a1h_ref[:, group * LANES : (group + 1) * LANES] = hi.astype(jnp.bfloat16)
        a1l_ref[:, group * LANES : (group + 1) * LANES] = low.astype(jnp.bfloat16)
    earlier = [name[0:QUARTER] for name in names[:8]]
    for group in range(2):
        earlier += [names[4 * group + (p - 1) % 4][QUARTER : 2 * QUARTER] for p in range(4)]
    code = gathered(codes, 0, 2, 32)
    gram = gathered(gram_hi, 0, 2, 96) + gathered(gram_lo, 0, 2, 32)
    put_split(a2h_ref, a2l_ref, listed(jnp.concatenate(earlier, axis=0), code, gram))


def sweep_kernel(
    n, tm, recv_ref, sg_ref, own_ref, a1h_ref, a1l_ref, a2h_ref, a2l_ref, a3h_ref, a3l_ref, traces_ref, rms_ref
):
    me = lax.axis_index("tile")
    frames = 8 * tm
    block = lax.shift_right_logical(iota((frames, LANES), 1), 5)
    messages = []
    for rel in REACH:
        first = tile_at(me, rel, n) * tm
        messages.append(jnp.concatenate([recv_ref[first + t] for t in range(tm)], axis=0))

    def gathered(group, turn):
        out = messages[4 * group]
        for q in range(4):
            if q or turn:
                out = jnp.where(block == (q + turn) % 4, messages[4 * group + q], out)
        return out

    gram = sg_ref[0:1, :]
    first_lane = iota((1, LANES), 1)

    def gram_of(group, colour):
        rows = gathered(group, 3)[colour - 1 : colour]
        rows = pltpu.roll(rows, 64 if colour == 1 else 96, 1)
        if group:
            return rows
        own = lax.shift_right_logical(first_lane, 5) == colour
        return jnp.where(own, gram, rows)

    x0 = [gathered(group, 0) for group in range(3)]
    n1 = dot_split(jnp.concatenate(x0, axis=1), a1h_ref[...], a1l_ref[...])
    x1 = [
        jnp.maximum((gathered(g, 1) - n1[:, g * LANES : (g + 1) * LANES]) / gram_of(g, 1), 0.0) for g in range(2)
    ]
    n2 = dot_split(jnp.concatenate([x0[0], x0[1], x1[0], x1[1]], axis=1), a2h_ref[...], a2l_ref[...])
    x2 = jnp.maximum((gathered(0, 2) - n2) / gram_of(0, 2), 0.0)
    n3 = dot_split(jnp.concatenate([x0[0], x1[0], x2], axis=1), a3h_ref[...], a3l_ref[...])
    x3 = jnp.maximum((messages[0] - n3) / gram, 0.0)
    own = jnp.where(
        block == 0, messages[0], jnp.where(block == 1, x1[0], jnp.where(block == 2, x2, x3))
    )
    energy = jnp.sum(own * own, axis=0, keepdims=True)
    half = lax.axis_index("tm")
    mine = own[0:8]
    for t in range(1, tm):
        mine = jnp.where(half == t, own[8 * t : 8 * t + 8], mine)
    order = (iota((LANES, LANES), 0).astype(jnp.float32) == own_ref[16:17, :]).astype(jnp.bfloat16)
    stacked = jnp.concatenate([mine, jnp.broadcast_to(energy, (8, LANES))], axis=0)
    placed = join3(dot(split3(stacked), order))
    traces_ref[...] = placed[0:8]
    rms_ref[...] = jnp.sqrt(placed[8:9] / frames + 1e-06)


def shards(
    data, send_list, footprint_slot, footprint, colour, correlation, correlation_gram, traces_init
):
    n = lax.axis_size("tile")
    tm = lax.axis_size("tm")
    f32, bf16 = jnp.float32, jnp.bfloat16
    shape = jax.ShapeDtypeStruct
    vmem = pl.BlockSpec(memory_space=pltpu.VMEM)
    hbm = pl.BlockSpec(memory_space=pltpu.HBM)

    def call(body, outs, ins, scratch=(), limit=VMEM_LIMIT):
        return pl.pallas_call(
            body,
            out_shape=outs,
            in_specs=ins,
            out_specs=[vmem] * len(outs),
            scratch_shapes=scratch,
            compiler_params=pltpu.CompilerParams(vmem_limit_bytes=limit),
        )

    inputs = (
        send_list[0].T, data, colour.reshape(1, LANES), correlation.T, correlation_gram.T, traces_init,
        footprint_slot.T,
    )
    outgoing, own = call(
        functools.partial(pack_kernel, n),
        [shape((n, DATA_ROWS + META_ROWS, LANES), bf16), shape((32, LANES), f32)],
        [hbm] * 7,
        [pltpu.SMEM(inputs[0].shape, jnp.int32)]
        + [pltpu.VMEM(x.shape, x.dtype) for x in inputs[1:]]
        + [pltpu.SemaphoreType.DMA((7,))],
        PACK_LIMIT,
    )(*[pltpu.with_memory_space_constraint(x, pltpu.HBM) for x in inputs])
    arrived = lax.all_to_all(outgoing, "tile", split_axis=0, concat_axis=0, tiled=True)
    message, self_gram, a3h, a3l = call(
        functools.partial(project_kernel, n, tm),
        [shape((n * tm, 8, LANES), f32), shape((8, LANES), f32)] + [shape((384, LANES), bf16)] * 2,
        [vmem] * 3,
    )(arrived, footprint.reshape(8 * LANES, LANES), own)
    messages = lax.all_to_all(message, ("tile", "tm"), split_axis=0, concat_axis=0, tiled=True)
    a1h, a1l, a2h, a2l = call(
        functools.partial(coef_kernel, n),
        [shape((384, 2 * LANES), bf16)] * 2 + [shape((512, LANES), bf16)] * 2,
        [vmem],
    )(arrived)
    traces, rms = call(
        functools.partial(sweep_kernel, n, tm),
        [shape((8, LANES), f32), shape((1, LANES), f32)],
        [vmem] * 9,
    )(messages, self_gram, own, a1h, a1l, a2h, a2l, a3h, a3l)
    return (traces, rms.reshape(LANES))


def solution(mesh):
    placed = (
        P("tile", "tm", None),
        P("tile", None, None),
        P("tile", None),
        P("tile", None, None),
        P("tile"),
        P("tile", None),
        P("tile", None),
        P("tm", "tile"),
    )
    return jax.shard_map(
        shards, mesh=mesh, in_specs=placed, out_specs=(P("tm", "tile"), P("tile")), check_vma=False
    )
```

```python
import functools

import jax
import jax.numpy as jnp
from jax import lax
from jax.experimental import pallas as pl
from jax.experimental.pallas import tpu as pltpu
from jax.sharding import PartitionSpec as P

REACH = (
    (0, 0), (1, 0), (-1, 0), (0, 1),
    (1, 1), (-1, 1), (2, 0), (-2, 0),
    (3, 0), (-3, 0), (2, 1), (-2, 1),
)
NEAR = REACH[:4]
LANES = 128
QUARTER = 32
DATA_ROWS = 64
META_ROWS = 32
GROUP = 4
VMEM_LIMIT = 48 * 2 ** 20
PACK_LIMIT = 48 * 2 ** 20
NT = (((1,), (1,)), ((), ()))


def iota(shape, dim):
    return lax.broadcasted_iota(jnp.int32, shape, dim)


def reach_at(device, near):
    return REACH.index((device[0] + near[0], (device[1] + near[1]) % 2))


def tile_at(me, rel, n):
    return lax.rem(me + rel[0] + rel[1] * (n // 2) + n, n)


def dot(a, b):
    return jnp.dot(a, b, preferred_element_type=jnp.float32)


def dot_nt(a, b):
    return lax.dot_general(a, b, NT, preferred_element_type=jnp.float32)


def split2(x):
    hi = x.astype(jnp.bfloat16).astype(jnp.float32)
    return hi, x - hi


def split3(x):
    hi, rest = split2(x)
    mid, low = split2(rest)
    return jnp.concatenate([hi, mid, low], axis=0).astype(jnp.bfloat16)


def places(colour_row):
    in_class = colour_row == iota((8, LANES), 0)
    before = (iota((LANES, LANES), 0) < iota((LANES, LANES), 1)).astype(jnp.bfloat16)
    counts = dot(in_class.astype(jnp.bfloat16), before)
    rank = jnp.sum(jnp.where(in_class, counts, 0.0), axis=0, keepdims=True)
    return rank + (colour_row * QUARTER).astype(jnp.float32)


def pack_kernel(n, *refs):
    sources, (out_ref, own_ref), held, sems = refs[:7], refs[7:9], refs[9:16], refs[16]
    send_ref, data_ref, colour_ref, corr_ref, gram_ref, init_ref, slot_ref = held
    copies = [pltpu.make_async_copy(a, b, sems.at[i]) for i, (a, b) in enumerate(zip(sources, held))]
    for copy in copies:
        copy.start()
    me = lax.axis_index("tile")
    lane = iota((8, LANES), 1)
    row = iota((8, LANES), 0)
    for copy in copies[2:]:
        copy.wait()
    own_ref[24:32, :] = slot_ref[...].astype(jnp.float32)
    pos = places(colour_ref[...])
    order = (iota((LANES, LANES), 0).astype(jnp.float32) == pos).astype(jnp.bfloat16)
    ids = corr_ref[...]
    away = jnp.bitwise_and(lax.shift_right_logical(ids, 7) - me, n - 1)
    which = jnp.where(away == 0, 0, jnp.where(away == 1, 1, jnp.where(away == n - 1, 2, 3)))
    code = which * LANES + jnp.bitwise_and(ids, LANES - 1) - 2 * LANES
    code = code.astype(jnp.float32)
    gram = gram_ref[...]
    gram_hi, gram_lo = split2(gram)
    init_hi, init_lo = split2(init_ref[...])
    rows = [code, gram_hi, gram_lo, lane.astype(jnp.float32)]
    placed = dot_nt(jnp.concatenate(rows, axis=0).astype(jnp.bfloat16), order)
    own_ref[0:8, :] = code
    own_ref[8:16, :] = gram
    own_ref[16:24, :] = jnp.broadcast_to(pos, (8, LANES))
    own_ref[32:40, :] = placed[24:32]
    first = jnp.where(lane < 64, pltpu.roll(placed[0:8], 96, 1), pltpu.roll(placed[8:16], 32, 1))
    spread = jnp.where(row == 0, pltpu.roll(jnp.broadcast_to(pos, (8, LANES)), 64, 1), pos)
    second = jnp.where(lane < 64, pltpu.roll(placed[16:24], 96, 1), spread)
    meta = jnp.concatenate([first, second, init_hi, init_lo], axis=0).astype(jnp.bfloat16)
    for copy in copies[:2]:
        copy.wait()
    for target in range(n):
        out_ref[target, DATA_ROWS:, :] = meta
        blocks = [data_ref[send_ref[c, target]].astype(jnp.float32) for c in range(8)]
        out_ref[target, :DATA_ROWS, :] = jnp.concatenate(blocks, axis=0).astype(jnp.bfloat16)


def lookup(table, index):
    return jnp.take_along_axis(table, index, axis=1)


def spread_row(rows, i):
    return jnp.broadcast_to(rows[i : i + 1], (8, LANES))


def pick(cases, which):
    out = cases[-1]
    for i in range(len(cases) - 1):
        out = jnp.where(which == i, cases[i], out)
    return out


def edges(devices, places_of, which, index, weight, sources):
    place, device = None, None
    for f in devices:
        found = lookup(places_of[f], index)
        place = found if place is None else jnp.where(which == f, found, place)
    place = place.astype(jnp.int32)
    colour = lax.shift_right_logical(place, 5)
    turn = jnp.bitwise_and(which + colour, 3)
    lanes = turn * QUARTER + jnp.bitwise_and(place, QUARTER - 1)
    tile = colour * 4 + lax.shift_right_logical(which, 2)
    return lanes, [jnp.where(tile == c * 4 + g, weight, 0.0) for c, g in sources]


SOURCES = (
    ((0, 0), (0, 1)),
    ((0, 0), (0, 1), (0, 2)),
    ((0, 0), (0, 1), (1, 0), (1, 1)),
    ((0, 0), (1, 0), (2, 0)),
)


def project_kernel(n, tm, recv_ref, fp_ref, own_ref, out_ref, gram_ref, lanes_ref, weights_ref, wide_ref):
    me = lax.axis_index("tile")
    lane = iota((8, LANES), 1)
    row = iota((8, LANES), 0)
    wide_ref[...] = fp_ref[...].astype(jnp.float32)
    weights, squares = [], None
    for j in range(8):
        rows = wide_ref[pl.ds(j, LANES, stride=8), :]
        weights.append(rows.astype(jnp.bfloat16))
        squares = rows * rows if j == 0 else squares + rows * rows
    weights = jnp.concatenate(weights, axis=0)
    gram = dot_nt(jnp.ones((8, LANES), jnp.bfloat16), split3(squares))
    gram = gram[:, :LANES] + gram[:, LANES : 2 * LANES] + gram[:, 2 * LANES :]
    slot_row = jnp.concatenate([own_ref[24 + j : 25 + j, :] for j in range(8)], axis=1)
    slot_row = jnp.broadcast_to(slot_row, (8, 8 * LANES))
    total = jnp.zeros((8, 8 * LANES), jnp.float32)
    for source in range(0, n, GROUP):
        blocks = recv_ref[source : source + GROUP, :DATA_ROWS, :].reshape(GROUP * DATA_ROWS, LANES)
        product = dot_nt(blocks, weights)
        for c in range(GROUP * 8):
            hit = slot_row == float(source * 8 + c)
            total = jnp.where(hit, product[8 * c : 8 * c + 8], total)
    projected = total[:, :LANES]
    for j in range(1, 8):
        projected = projected + total[:, j * LANES : (j + 1) * LANES]
    metas = [recv_ref[tile_at(me, rel, n), DATA_ROWS:, :].astype(jnp.float32) for rel in REACH]
    places_of = []
    for meta in metas:
        found = jnp.where(lane < 64, pltpu.roll(spread_row(meta, 8), 64, 1), spread_row(meta, 9))
        places_of.append(found)
    code = own_ref[0:8, :].astype(jnp.int32) + 2 * LANES
    index, which = jnp.bitwise_and(code, LANES - 1), lax.shift_right_logical(code, 7)
    place = pick([lookup(places_of[r], index) for r in range(4)], which).astype(jnp.int32)
    own_place = own_ref[16:24, :].astype(jnp.int32)
    after = lax.shift_right_logical(place, 5) > lax.shift_right_logical(own_place, 5)
    late = jnp.where(after, own_ref[8:16, :], 0.0)
    starts = [meta[16:24] + meta[24:32] for meta in metas[:4]]
    held = None
    for i in range(8):
        at, owner = spread_row(index, i), spread_row(which, i)
        term = pick([lookup(start, at) for start in starts], owner) * spread_row(late, i)
        held = term if held is None else held + term
    names = own_ref[32:40, :].astype(jnp.int32)
    base = lookup(projected - held, names)
    gram = lookup(gram, names)
    gram_ref[...] = gram
    message = jnp.where(lane < QUARTER, jnp.maximum(base / gram, 0.0), base)
    grams12 = jnp.where(row == 0, pltpu.roll(gram, 64, 1), pltpu.roll(gram, 32, 1))
    others = jnp.where(lane < 96, message, grams12)
    for t in range(n * tm):
        out_ref[t] = others
    for i, rel in enumerate(REACH):
        source = message if i == 0 else others
        turned = source if i % 4 == 0 else pltpu.roll(source, QUARTER * (i % 4), 1)
        target = tile_at(me, (-rel[0], rel[1]), n)
        for t in range(tm):
            out_ref[target * tm + t] = turned
    block = lax.shift_right_logical(lane, 5)
    codes = []
    for i in range(8):
        code = metas[i][0:8].astype(jnp.int32) + 2 * LANES
        at = [reach_at(REACH[i], near) for near in NEAR]
        device = pick(at, lax.shift_right_logical(code, 7))
        codes.append((device * LANES + jnp.bitwise_and(code, LANES - 1)).astype(jnp.float32))

    def gathered(parts, group, colour, start):
        out = None
        for q in range(4):
            p = (q + colour) % 4
            shift = (QUARTER * p - start) % LANES
            turned = parts[4 * group + q]
            turned = turned if shift == 0 else pltpu.roll(turned, shift, 1)
            out = turned if out is None else jnp.where(block == p, turned, out)
        return out

    hi, low = [meta[0:8] for meta in metas[:8]], [meta[8:16] for meta in metas[:8]]
    slot = 0
    for step, (group, colour) in enumerate(((0, 1), (1, 1), (0, 2), (0, 3))):
        if step < 3:
            start = QUARTER * (colour - 1)
            code = gathered(codes, group, colour, start).astype(jnp.int32)
            weight = gathered(hi, group, colour, start + 64) + gathered(low, group, colour, start)
            device, at = lax.shift_right_logical(code, 7), jnp.bitwise_and(code, LANES - 1)
            devices = range(12) if step == 1 else range(8)
        else:
            weight = lookup(own_ref[8:16, :], names)
            device, at = lookup(which, names), lookup(index, names)
            devices = range(4)
        lanes, parts = edges(devices, places_of, device, at, weight, SOURCES[step])
        lanes_ref[8 * step : 8 * step + 8, :] = lanes
        for part in parts:
            weights_ref[8 * slot : 8 * slot + 8, :] = part
            slot += 1


def sweep_kernel(n, tm, recv_ref, gram_ref, own_ref, lanes_ref, weights_ref, traces_ref, rms_ref):
    me = lax.axis_index("tile")
    half = lax.axis_index("tm")
    lane = iota((8, LANES), 1)
    block = lax.shift_right_logical(lane, 5)
    first = [tile_at(me, rel, n) * tm for rel in REACH]
    gram = gram_ref[...]

    def gathered(messages, group, turn):
        out = messages[4 * group]
        for q in range(4):
            if q or turn:
                out = jnp.where(block == (q + turn) % 4, messages[4 * group + q], out)
        return out

    def gram_of(messages, group, colour):
        rows = spread_row(gathered(messages, group, 3), colour - 1)
        rows = pltpu.roll(rows, 64 if colour == 1 else 96, 1)
        return jnp.where(block == colour, gram, rows) if group == 0 else rows

    def neighbours(step, tiles):
        slot = sum(len(sources) for sources in SOURCES[:step])
        total = None
        for i in range(8):
            at = jnp.broadcast_to(lanes_ref[8 * step + i : 8 * step + i + 1, :], (8, LANES))
            for s, tile in enumerate(tiles):
                place = 8 * (slot + s) + i
                term = lookup(tile, at) * weights_ref[place : place + 1, :]
                total = term if total is None else total + term
        return total

    energy, mine = None, None
    for t in range(tm):
        messages = [recv_ref[f + t] for f in first]
        x0 = [gathered(messages, group, 0) for group in range(3)]
        x1 = []
        for group in range(2):
            fresh = gathered(messages, group, 1) - neighbours(group, x0[: 2 + group])
            x1.append(jnp.maximum(fresh / gram_of(messages, group, 1), 0.0))
        fresh = gathered(messages, 0, 2) - neighbours(2, [x0[0], x0[1], x1[0], x1[1]])
        x2 = jnp.maximum(fresh / gram_of(messages, 0, 2), 0.0)
        fresh = messages[0] - neighbours(3, [x0[0], x1[0], x2])
        x3 = jnp.maximum(fresh / gram, 0.0)
        own = pick([messages[0], x1[0], x2, x3], block)
        square = jnp.sum(own * own, axis=0, keepdims=True)
        energy = square if energy is None else energy + square
        mine = own if mine is None else jnp.where(half == t, own, mine)
    order = own_ref[16:24, :].astype(jnp.int32)
    traces_ref[...] = lookup(mine, order)
    energy = lookup(jnp.broadcast_to(energy, (8, LANES)), order)
    rms_ref[...] = jnp.sqrt(energy[0:1] / (8 * tm) + 1e-06)


def shards(
    data, send_list, footprint_slot, footprint, colour, correlation, correlation_gram, traces_init
):
    n = lax.axis_size("tile")
    tm = lax.axis_size("tm")
    f32, bf16 = jnp.float32, jnp.bfloat16
    shape = jax.ShapeDtypeStruct
    vmem = pl.BlockSpec(memory_space=pltpu.VMEM)
    hbm = pl.BlockSpec(memory_space=pltpu.HBM)

    def call(body, outs, ins, scratch=(), limit=VMEM_LIMIT):
        return pl.pallas_call(
            body,
            out_shape=outs,
            in_specs=ins,
            out_specs=[vmem] * len(outs),
            scratch_shapes=scratch,
            compiler_params=pltpu.CompilerParams(vmem_limit_bytes=limit),
        )

    inputs = (
        send_list[0].T, data, colour.reshape(1, LANES), correlation.T, correlation_gram.T, traces_init,
        footprint_slot.T,
    )
    outgoing, own = call(
        functools.partial(pack_kernel, n),
        [shape((n, DATA_ROWS + META_ROWS, LANES), bf16), shape((40, LANES), f32)],
        [hbm] * 7,
        [pltpu.SMEM(inputs[0].shape, jnp.int32)]
        + [pltpu.VMEM(x.shape, x.dtype) for x in inputs[1:]]
        + [pltpu.SemaphoreType.DMA((7,))],
        PACK_LIMIT,
    )(*[pltpu.with_memory_space_constraint(x, pltpu.HBM) for x in inputs])
    arrived = lax.all_to_all(outgoing, "tile", split_axis=0, concat_axis=0, tiled=True)
    slots = sum(len(sources) for sources in SOURCES)
    message, gram, lanes, weights = call(
        functools.partial(project_kernel, n, tm),
        [shape((n * tm, 8, LANES), f32), shape((8, LANES), f32)]
        + [shape((8 * len(SOURCES), LANES), jnp.int32), shape((8 * slots, LANES), f32)],
        [vmem] * 3,
        [pltpu.VMEM((8 * LANES, LANES), f32)],
    )(arrived, footprint.reshape(8 * LANES, LANES), own)
    messages = lax.all_to_all(message, ("tile", "tm"), split_axis=0, concat_axis=0, tiled=True)
    traces, rms = call(
        functools.partial(sweep_kernel, n, tm),
        [shape((8, LANES), f32), shape((1, LANES), f32)],
        [vmem] * 5,
    )(messages, gram, own, lanes, weights)
    return (traces, rms.reshape(LANES))


def solution(mesh):
    placed = (
        P("tile", "tm", None),
        P("tile", None, None),
        P("tile", None),
        P("tile", None, None),
        P("tile"),
        P("tile", None),
        P("tile", None),
        P("tm", "tile"),
    )
    return jax.shard_map(
        shards, mesh=mesh, in_specs=placed, out_specs=(P("tm", "tile"), P("tile")), check_vma=False
    )
```

```python
import functools

import jax
import jax.numpy as jnp
from jax import lax
from jax.experimental import pallas as pl
from jax.experimental.pallas import tpu as pltpu
from jax.sharding import PartitionSpec as P

REACH = (
    (0, 0), (1, 0), (-1, 0), (0, 1),
    (1, 1), (-1, 1), (2, 0), (-2, 0),
    (3, 0), (-3, 0), (2, 1), (-2, 1),
)
NEAR = REACH[:4]
LANES = 128
QUARTER = 32
DATA_ROWS = 64
META_ROWS = 24
LOW_SENT = 6
GROUP = 4
VMEM_LIMIT = 48 * 2 ** 20
PACK_LIMIT = 48 * 2 ** 20
NT = (((1,), (1,)), ((), ()))


def iota(shape, dim):
    return lax.broadcasted_iota(jnp.int32, shape, dim)


def reach_at(device, near):
    return REACH.index((device[0] + near[0], (device[1] + near[1]) % 2))


def tile_at(me, rel, n):
    return lax.rem(me + rel[0] + rel[1] * (n // 2) + n, n)


def dot(a, b):
    return jnp.dot(a, b, preferred_element_type=jnp.float32)


def dot_nt(a, b):
    return lax.dot_general(a, b, NT, preferred_element_type=jnp.float32)


def split2(x):
    hi = x.astype(jnp.bfloat16).astype(jnp.float32)
    return hi, x - hi


def split3(x):
    hi, rest = split2(x)
    mid, low = split2(rest)
    return jnp.concatenate([hi, mid, low], axis=0).astype(jnp.bfloat16)


def places(colour_row):
    in_class = colour_row == iota((8, LANES), 0)
    before = (iota((LANES, LANES), 0) < iota((LANES, LANES), 1)).astype(jnp.bfloat16)
    counts = dot(in_class.astype(jnp.bfloat16), before)
    rank = jnp.sum(jnp.where(in_class, counts, 0.0), axis=0, keepdims=True)
    return rank + (colour_row * QUARTER).astype(jnp.float32)


def pack_kernel(n, *refs):
    sources, (out_ref, own_ref), held, sems = refs[:7], refs[7:9], refs[9:16], refs[16]
    colour_ref, corr_ref, gram_ref, init_ref, slot_ref, send_ref, data_ref = held
    copies = [pltpu.make_async_copy(a, b, sems.at[i]) for i, (a, b) in enumerate(zip(sources, held))]
    for copy in copies:
        copy.start()
    me = lax.axis_index("tile")
    lane = iota((8, LANES), 1)
    row = iota((8, LANES), 0)
    for copy in copies[:5]:
        copy.wait()
    own_ref[24:32, :] = slot_ref[...].astype(jnp.float32)
    pos = places(colour_ref[...])
    order = (iota((LANES, LANES), 0).astype(jnp.float32) == pos).astype(jnp.bfloat16)
    ids = corr_ref[...]
    away = jnp.bitwise_and(lax.shift_right_logical(ids, 7) - me, n - 1)
    which = jnp.where(away == 0, 0, jnp.where(away == 1, 1, jnp.where(away == n - 1, 2, 3)))
    code = which * LANES + jnp.bitwise_and(ids, LANES - 1) - 2 * LANES
    code = code.astype(jnp.float32)
    gram = gram_ref[...]
    gram_hi, gram_lo = split2(gram)
    init_hi, init_lo = split2(init_ref[...])
    rows = [code, gram_hi, gram_lo, init_hi, init_lo, lane.astype(jnp.float32)]
    placed = dot_nt(jnp.concatenate(rows, axis=0).astype(jnp.bfloat16), order)
    placed = [placed[8 * i : 8 * i + 8] for i in range(6)]
    pos = jnp.broadcast_to(pos, (8, LANES))
    own_ref[0:8, :] = code
    own_ref[8:16, :] = gram
    own_ref[16:24, :] = pos
    own_ref[32:40, :] = placed[5]
    first = jnp.where(lane < 64, pltpu.roll(placed[0], 96, 1), pltpu.roll(placed[1], 32, 1))
    tails = []
    for low, even, odd in ((64, 96, 64), (32, 32, 0)):
        even = pltpu.roll(pos, even, 1)
        odd = pltpu.roll(pos, odd, 1) if odd else pos
        tails.append(
            jnp.where(row < LOW_SENT, pltpu.roll(placed[2], low, 1), jnp.where(row == LOW_SENT, even, odd))
        )
    second = jnp.where(lane < 96, pltpu.roll(placed[3], 96, 1), tails[0])
    third = jnp.where(lane < 96, pltpu.roll(placed[4], 96, 1), tails[1])
    meta = jnp.concatenate([first, second, third], axis=0)
    for copy in copies[5:]:
        copy.wait()
    for target in range(n):
        blocks = [data_ref[send_ref[c, target]].astype(jnp.float32) for c in range(8)]
        out_ref[target] = jnp.concatenate(blocks + [meta], axis=0).astype(jnp.bfloat16)


def lookup(table, index):
    return jnp.take_along_axis(table, index, axis=1)


def spread_row(rows, i):
    return jnp.broadcast_to(rows[i : i + 1], (8, LANES))


def pick(cases, which):
    out = cases[-1]
    for i in range(len(cases) - 1):
        out = jnp.where(which == i, cases[i], out)
    return out


def edges(devices, places_of, which, index, weight, sources):
    place, device = None, None
    for f in devices:
        found = lookup(places_of[f], index)
        place = found if place is None else jnp.where(which == f, found, place)
    place = place.astype(jnp.int32)
    colour = lax.shift_right_logical(place, 5)
    turn = jnp.bitwise_and(which + colour, 3)
    lanes = turn * QUARTER + jnp.bitwise_and(place, QUARTER - 1)
    tile = colour * 4 + lax.shift_right_logical(which, 2)
    return lanes, [jnp.where(tile == c * 4 + g, weight, 0.0) for c, g in sources]


SOURCES = (
    ((0, 0), (0, 1)),
    ((0, 0), (0, 1), (0, 2)),
    ((0, 0), (0, 1), (1, 0), (1, 1)),
    ((0, 0), (1, 0), (2, 0)),
)


def project_kernel(n, tm, recv_ref, fp_ref, own_ref, out_ref, gram_ref, lanes_ref, weights_ref, wide_ref):
    me = lax.axis_index("tile")
    lane = iota((8, LANES), 1)
    row = iota((8, LANES), 0)
    wide_ref[...] = fp_ref[...].astype(jnp.float32)
    weights, squares = [], None
    for j in range(8):
        rows = wide_ref[pl.ds(j, LANES, stride=8), :]
        weights.append(rows.astype(jnp.bfloat16))
        squares = rows * rows if j == 0 else squares + rows * rows
    weights = jnp.concatenate(weights, axis=0)
    gram = dot_nt(jnp.ones((8, LANES), jnp.bfloat16), split3(squares))
    gram = gram[:, :LANES] + gram[:, LANES : 2 * LANES] + gram[:, 2 * LANES :]
    slot_row = jnp.concatenate([own_ref[24 + j : 25 + j, :] for j in range(8)], axis=1)
    slot_row = jnp.broadcast_to(slot_row, (8, 8 * LANES))
    total = jnp.zeros((8, 8 * LANES), jnp.float32)
    for source in range(0, n, GROUP):
        blocks = recv_ref[source : source + GROUP, :DATA_ROWS, :].reshape(GROUP * DATA_ROWS, LANES)
        product = dot_nt(blocks, weights)
        for c in range(GROUP * 8):
            hit = slot_row == float(source * 8 + c)
            total = jnp.where(hit, product[8 * c : 8 * c + 8], total)
    projected = total[:, :LANES]
    for j in range(1, 8):
        projected = projected + total[:, j * LANES : (j + 1) * LANES]
    block = lax.shift_right_logical(lane, 5)
    metas = [recv_ref[tile_at(me, rel, n)].astype(jnp.float32)[DATA_ROWS:] for rel in REACH]
    places_of = []
    for meta in metas:
        parts = [spread_row(meta, 8 + LOW_SENT), spread_row(meta, 9 + LOW_SENT)]
        parts += [spread_row(meta, 16 + LOW_SENT), spread_row(meta, 17 + LOW_SENT)]
        parts = [pltpu.roll(part, 32 * i + 32, 1) if i < 3 else part for i, part in enumerate(parts)]
        places_of.append(pick(parts, block))
    code = own_ref[0:8, :].astype(jnp.int32) + 2 * LANES
    index, which = jnp.bitwise_and(code, LANES - 1), lax.shift_right_logical(code, 7)
    place = pick([lookup(places_of[r], index) for r in range(4)], which).astype(jnp.int32)
    own_place = own_ref[16:24, :].astype(jnp.int32)
    after = lax.shift_right_logical(place, 5) > lax.shift_right_logical(own_place, 5)
    late = jnp.where(after, own_ref[8:16, :], 0.0)
    starts = [pltpu.roll(meta[8:16] + meta[16:24], 32, 1) for meta in metas[:4]]
    held = None
    for i in range(8):
        at, owner = spread_row(place, i), spread_row(which, i)
        term = pick([lookup(start, at) for start in starts], owner) * spread_row(late, i)
        held = term if held is None else held + term
    names = own_ref[32:40, :].astype(jnp.int32)
    base = lookup(projected - held, names)
    gram = lookup(gram, names)
    gram_ref[...] = gram
    message = jnp.where(lane < QUARTER, jnp.maximum(base / gram, 0.0), base)
    listed = lookup(own_ref[8:16, :], names)
    rest = split2(listed)[1]
    spare = jnp.where(row < 4, spread_row(rest, LOW_SENT), spread_row(rest, LOW_SENT + 1))
    spare = jnp.where(row < 2, gram, spare)
    spare = jnp.where(jnp.bitwise_and(row, 1) == 0, pltpu.roll(spare, 64, 1), pltpu.roll(spare, 32, 1))
    others = jnp.where(lane < 96, message, spare)
    for t in range(n * tm):
        out_ref[t] = others
    for i, rel in enumerate(REACH):
        source = message if i == 0 else others
        turned = source if i % 4 == 0 else pltpu.roll(source, QUARTER * (i % 4), 1)
        target = tile_at(me, (-rel[0], rel[1]), n)
        for t in range(tm):
            out_ref[target * tm + t] = turned
    codes = []
    for i in range(8):
        code = metas[i][0:8].astype(jnp.int32) + 2 * LANES
        at = [reach_at(REACH[i], near) for near in NEAR]
        device = pick(at, lax.shift_right_logical(code, 7))
        codes.append((device * LANES + jnp.bitwise_and(code, LANES - 1)).astype(jnp.float32))

    def gathered(parts, group, colour, start):
        out = None
        for q in range(4):
            p = (q + colour) % 4
            shift = (QUARTER * p - start) % LANES
            turned = parts[4 * group + q]
            turned = turned if shift == 0 else pltpu.roll(turned, shift, 1)
            out = turned if out is None else jnp.where(block == p, turned, out)
        return out

    high = [meta[0:8] for meta in metas[:8]]
    slot = 0
    for step, (group, colour) in enumerate(((0, 1), (1, 1), (0, 2), (0, 3))):
        if step < 3:
            start = QUARTER * (colour - 1)
            code = gathered(codes, group, colour, start).astype(jnp.int32)
            low = [jnp.where(row < LOW_SENT, meta[8 * colour : 8 * colour + 8], 0.0) for meta in metas[:8]]
            weight = gathered(high, group, colour, start + 64) + gathered(low, group, colour, 96)
            if group == 0:
                weight = jnp.where(block == colour, listed, weight)
            device, at = lax.shift_right_logical(code, 7), jnp.bitwise_and(code, LANES - 1)
            devices = range(12) if step == 1 else range(8)
        else:
            weight = listed
            device, at = lookup(which, names), lookup(index, names)
            devices = range(4)
        lanes, parts = edges(devices, places_of, device, at, weight, SOURCES[step])
        lanes_ref[8 * step : 8 * step + 8, :] = lanes
        for part in parts:
            weights_ref[8 * slot : 8 * slot + 8, :] = part
            slot += 1


def sweep_kernel(n, tm, recv_ref, gram_ref, own_ref, lanes_ref, weights_ref, traces_ref, rms_ref):
    me = lax.axis_index("tile")
    half = lax.axis_index("tm")
    lane = iota((8, LANES), 1)
    block = lax.shift_right_logical(lane, 5)
    first = [tile_at(me, rel, n) * tm for rel in REACH]
    gram = gram_ref[...]

    def gathered(messages, group, turn):
        out = messages[4 * group]
        for q in range(4):
            if q or turn:
                out = jnp.where(block == (q + turn) % 4, messages[4 * group + q], out)
        return out

    def spare_of(messages, group, colour):
        return pltpu.roll(gathered(messages, group, 3), 64 if colour == 1 else 96, 1)

    def gram_of(spare, group, colour):
        rows = spread_row(spare, colour - 1)
        return jnp.where(block == colour, gram, rows) if group == 0 else rows

    def neighbours(step, tiles, spare, group, colour):
        slot = sum(len(sources) for sources in SOURCES[:step])
        total = None
        for i in range(8):
            at = jnp.broadcast_to(lanes_ref[8 * step + i : 8 * step + i + 1, :], (8, LANES))
            for s, tile in enumerate(tiles):
                place = 8 * (slot + s) + i
                weight = jnp.broadcast_to(weights_ref[place : place + 1, :], (8, LANES))
                if spare is not None and i >= LOW_SENT:
                    low = spread_row(spare, 2 * (i - LOW_SENT) + 1 + colour)
                    low = jnp.where(block == colour, 0.0, low) if group == 0 else low
                    weight = jnp.where(weight != 0.0, weight + low, 0.0)
                term = lookup(tile, at) * weight
                total = term if total is None else total + term
        return total

    energy, mine = None, None
    for t in range(tm):
        messages = [recv_ref[f + t] for f in first]
        x0 = [gathered(messages, group, 0) for group in range(3)]
        x1 = []
        for group in range(2):
            spare = spare_of(messages, group, 1)
            fresh = gathered(messages, group, 1) - neighbours(group, x0[: 2 + group], spare, group, 1)
            x1.append(jnp.maximum(fresh / gram_of(spare, group, 1), 0.0))
        spare = spare_of(messages, 0, 2)
        fresh = gathered(messages, 0, 2) - neighbours(2, [x0[0], x0[1], x1[0], x1[1]], spare, 0, 2)
        x2 = jnp.maximum(fresh / gram_of(spare, 0, 2), 0.0)
        fresh = messages[0] - neighbours(3, [x0[0], x1[0], x2], None, 0, 3)
        x3 = jnp.maximum(fresh / gram, 0.0)
        own = pick([messages[0], x1[0], x2, x3], block)
        square = jnp.sum(own * own, axis=0, keepdims=True)
        energy = square if energy is None else energy + square
        mine = own if mine is None else jnp.where(half == t, own, mine)
    order = own_ref[16:24, :].astype(jnp.int32)
    traces_ref[...] = lookup(mine, order)
    energy = lookup(jnp.broadcast_to(energy, (8, LANES)), order)
    rms_ref[...] = jnp.sqrt(energy[0:1] / (8 * tm) + 1e-06)


def shards(
    data, send_list, footprint_slot, footprint, colour, correlation, correlation_gram, traces_init
):
    n = lax.axis_size("tile")
    tm = lax.axis_size("tm")
    f32, bf16 = jnp.float32, jnp.bfloat16
    shape = jax.ShapeDtypeStruct
    vmem = pl.BlockSpec(memory_space=pltpu.VMEM)
    hbm = pl.BlockSpec(memory_space=pltpu.HBM)

    def call(body, outs, ins, scratch=(), limit=VMEM_LIMIT):
        return pl.pallas_call(
            body,
            out_shape=outs,
            in_specs=ins,
            out_specs=[vmem] * len(outs),
            scratch_shapes=scratch,
            compiler_params=pltpu.CompilerParams(vmem_limit_bytes=limit),
        )

    inputs = (
        colour.reshape(1, LANES), correlation.T, correlation_gram.T, traces_init, footprint_slot.T,
        send_list[0].T, data,
    )
    outgoing, own = call(
        functools.partial(pack_kernel, n),
        [shape((n, DATA_ROWS + META_ROWS, LANES), bf16), shape((40, LANES), f32)],
        [hbm] * 7,
        [pltpu.VMEM(x.shape, x.dtype) for x in inputs[:5]]
        + [pltpu.SMEM(inputs[5].shape, jnp.int32), pltpu.VMEM(data.shape, bf16)]
        + [pltpu.SemaphoreType.DMA((7,))],
        PACK_LIMIT,
    )(*[pltpu.with_memory_space_constraint(x, pltpu.HBM) for x in inputs])
    arrived = lax.all_to_all(outgoing, "tile", split_axis=0, concat_axis=0, tiled=True)
    slots = sum(len(sources) for sources in SOURCES)
    message, gram, lanes, weights = call(
        functools.partial(project_kernel, n, tm),
        [shape((n * tm, 8, LANES), f32), shape((8, LANES), f32)]
        + [shape((8 * len(SOURCES), LANES), jnp.int32), shape((8 * slots, LANES), f32)],
        [vmem] * 3,
        [pltpu.VMEM((8 * LANES, LANES), f32)],
    )(arrived, footprint.reshape(8 * LANES, LANES), own)
    messages = lax.all_to_all(message, ("tile", "tm"), split_axis=0, concat_axis=0, tiled=True)
    traces, rms = call(
        functools.partial(sweep_kernel, n, tm),
        [shape((8, LANES), f32), shape((1, LANES), f32)],
        [vmem] * 5,
    )(messages, gram, own, lanes, weights)
    return (traces, rms.reshape(LANES))


def solution(mesh):
    placed = (
        P("tile", "tm", None),
        P("tile", None, None),
        P("tile", None),
        P("tile", None, None),
        P("tile"),
        P("tile", None),
        P("tile", None),
        P("tm", "tile"),
    )
    return jax.shard_map(
        shards, mesh=mesh, in_specs=placed, out_specs=(P("tm", "tile"), P("tile")), check_vma=False
    )
```

```python
import functools

import jax
import jax.numpy as jnp
from jax import lax
from jax.experimental import pallas as pl
from jax.experimental.pallas import tpu as pltpu
from jax.sharding import PartitionSpec as P

REACH = (
    (0, 0), (1, 0), (-1, 0), (0, 1),
    (1, 1), (-1, 1), (2, 0), (-2, 0),
    (3, 0), (-3, 0), (2, 1), (-2, 1),
)
NEAR = REACH[:4]
ORDERS = {
    (16, 2): (
        [5, 0, 9, 8, 14, 2, 4, 12, 3, 1, 11, 10, 6, 7, 13, 15],
        [0, 17, 26, 21, 1, 25, 7, 24, 29, 9, 16, 5, 22, 12, 18, 8]
        + [13, 20, 28, 14, 19, 3, 2, 4, 23, 31, 27, 10, 6, 11, 15, 30],
    ),
}
LANES = 128
QUARTER = 32
DATA_ROWS = 64
META_ROWS = 24
LOW_SENT = 6
GROUP = 4
VMEM_LIMIT = 48 * 2 ** 20
PACK_LIMIT = 48 * 2 ** 20
NT = (((1,), (1,)), ((), ()))


def iota(shape, dim):
    return lax.broadcasted_iota(jnp.int32, shape, dim)


def reach_at(device, near):
    return REACH.index((device[0] + near[0], (device[1] + near[1]) % 2))


def tile_at(me, rel, n):
    return lax.rem(me + rel[0] + rel[1] * (n // 2) + n, n)


def slots_of(order):
    return [order.index(device) for device in range(len(order))]


def entry(table, i):
    if table == list(range(len(table))):
        return i
    words = [sum(table[w + b] << (8 * b) for b in range(4)) for w in range(0, len(table), 4)]
    word, at = words[0], lax.shift_right_logical(i, 2)
    for w in range(1, len(words)):
        word = jnp.where(at == w, words[w], word)
    return jnp.bitwise_and(lax.shift_right_logical(word, 8 * jnp.bitwise_and(i, 3)), 255)


def dot(a, b):
    return jnp.dot(a, b, preferred_element_type=jnp.float32)


def dot_nt(a, b):
    return lax.dot_general(a, b, NT, preferred_element_type=jnp.float32)


def split2(x):
    hi = x.astype(jnp.bfloat16).astype(jnp.float32)
    return hi, x - hi


def split3(x):
    hi, rest = split2(x)
    mid, low = split2(rest)
    return jnp.concatenate([hi, mid, low], axis=0).astype(jnp.bfloat16)


def places(colour_row):
    in_class = colour_row == iota((8, LANES), 0)
    before = (iota((LANES, LANES), 0) < iota((LANES, LANES), 1)).astype(jnp.bfloat16)
    counts = dot(in_class.astype(jnp.bfloat16), before)
    rank = jnp.sum(jnp.where(in_class, counts, 0.0), axis=0, keepdims=True)
    return rank + (colour_row * QUARTER).astype(jnp.float32)


def pack_kernel(n, slots, *refs):
    sources, (out_ref, own_ref), held, sems = refs[:7], refs[7:9], refs[9:16], refs[16]
    colour_ref, corr_ref, gram_ref, init_ref, slot_ref, send_ref, data_ref = held
    copies = [pltpu.make_async_copy(a, b, sems.at[i]) for i, (a, b) in enumerate(zip(sources, held))]
    for copy in copies:
        copy.start()
    me = lax.axis_index("tile")
    lane = iota((8, LANES), 1)
    row = iota((8, LANES), 0)
    for copy in copies[:5]:
        copy.wait()
    own_ref[24:32, :] = slot_ref[...].astype(jnp.float32)
    pos = places(colour_ref[...])
    order = (iota((LANES, LANES), 0).astype(jnp.float32) == pos).astype(jnp.bfloat16)
    ids = corr_ref[...]
    away = jnp.bitwise_and(lax.shift_right_logical(ids, 7) - me, n - 1)
    which = jnp.where(away == 0, 0, jnp.where(away == 1, 1, jnp.where(away == n - 1, 2, 3)))
    code = which * LANES + jnp.bitwise_and(ids, LANES - 1) - 2 * LANES
    code = code.astype(jnp.float32)
    gram = gram_ref[...]
    gram_hi, gram_lo = split2(gram)
    init_hi, init_lo = split2(init_ref[...])
    rows = [code, gram_hi, gram_lo, init_hi, init_lo, lane.astype(jnp.float32)]
    placed = dot_nt(jnp.concatenate(rows, axis=0).astype(jnp.bfloat16), order)
    placed = [placed[8 * i : 8 * i + 8] for i in range(6)]
    pos = jnp.broadcast_to(pos, (8, LANES))
    own_ref[0:8, :] = code
    own_ref[8:16, :] = gram
    own_ref[16:24, :] = pos
    own_ref[32:40, :] = placed[5]
    first = jnp.where(lane < 64, pltpu.roll(placed[0], 96, 1), pltpu.roll(placed[1], 32, 1))
    tails = []
    for low, even, odd in ((64, 96, 64), (32, 32, 0)):
        even = pltpu.roll(pos, even, 1)
        odd = pltpu.roll(pos, odd, 1) if odd else pos
        tails.append(
            jnp.where(row < LOW_SENT, pltpu.roll(placed[2], low, 1), jnp.where(row == LOW_SENT, even, odd))
        )
    second = jnp.where(lane < 96, pltpu.roll(placed[3], 96, 1), tails[0])
    third = jnp.where(lane < 96, pltpu.roll(placed[4], 96, 1), tails[1])
    meta = jnp.concatenate([first, second, third], axis=0)
    for copy in copies[5:]:
        copy.wait()
    for target in range(n):
        blocks = [data_ref[send_ref[c, target]].astype(jnp.float32) for c in range(8)]
        out_ref[slots[target]] = jnp.concatenate(blocks + [meta], axis=0).astype(jnp.bfloat16)


def lookup(table, index):
    return jnp.take_along_axis(table, index, axis=1)


def spread_row(rows, i):
    return jnp.broadcast_to(rows[i : i + 1], (8, LANES))


def pick(cases, which):
    out = cases[-1]
    for i in range(len(cases) - 1):
        out = jnp.where(which == i, cases[i], out)
    return out


def edges(devices, places_of, which, index, weight, sources):
    place, device = None, None
    for f in devices:
        found = lookup(places_of[f], index)
        place = found if place is None else jnp.where(which == f, found, place)
    place = place.astype(jnp.int32)
    colour = lax.shift_right_logical(place, 5)
    turn = jnp.bitwise_and(which + colour, 3)
    lanes = turn * QUARTER + jnp.bitwise_and(place, QUARTER - 1)
    tile = colour * 4 + lax.shift_right_logical(which, 2)
    return lanes, [jnp.where(tile == c * 4 + g, weight, 0.0) for c, g in sources]


SOURCES = (
    ((0, 0), (0, 1)),
    ((0, 0), (0, 1), (0, 2)),
    ((0, 0), (0, 1), (1, 0), (1, 1)),
    ((0, 0), (1, 0), (2, 0)),
)


def project_kernel(n, tm, slots, message_slots, recv_ref, fp_ref, own_ref, out_ref, gram_ref, lanes_ref, weights_ref, wide_ref):
    me = lax.axis_index("tile")
    lane = iota((8, LANES), 1)
    row = iota((8, LANES), 0)
    wide_ref[...] = fp_ref[...].astype(jnp.float32)
    weights, squares = [], None
    for j in range(8):
        rows = wide_ref[pl.ds(j, LANES, stride=8), :]
        weights.append(rows.astype(jnp.bfloat16))
        squares = rows * rows if j == 0 else squares + rows * rows
    weights = jnp.concatenate(weights, axis=0)
    gram = dot_nt(jnp.ones((8, LANES), jnp.bfloat16), split3(squares))
    gram = gram[:, :LANES] + gram[:, LANES : 2 * LANES] + gram[:, 2 * LANES :]
    slot_row = jnp.concatenate([own_ref[24 + j : 25 + j, :] for j in range(8)], axis=1)
    slot_row = jnp.broadcast_to(slot_row, (8, 8 * LANES))
    total = jnp.zeros((8, 8 * LANES), jnp.float32)
    for source in range(0, n, GROUP):
        blocks = [recv_ref[slots[source + i], :DATA_ROWS, :] for i in range(GROUP)]
        blocks = jnp.concatenate(blocks, axis=0)
        product = dot_nt(blocks, weights)
        for c in range(GROUP * 8):
            hit = slot_row == float(source * 8 + c)
            total = jnp.where(hit, product[8 * c : 8 * c + 8], total)
    projected = total[:, :LANES]
    for j in range(1, 8):
        projected = projected + total[:, j * LANES : (j + 1) * LANES]
    block = lax.shift_right_logical(lane, 5)
    metas = [recv_ref[entry(slots, tile_at(me, rel, n))].astype(jnp.float32)[DATA_ROWS:] for rel in REACH]
    places_of = []
    for meta in metas:
        parts = [spread_row(meta, 8 + LOW_SENT), spread_row(meta, 9 + LOW_SENT)]
        parts += [spread_row(meta, 16 + LOW_SENT), spread_row(meta, 17 + LOW_SENT)]
        parts = [pltpu.roll(part, 32 * i + 32, 1) if i < 3 else part for i, part in enumerate(parts)]
        places_of.append(pick(parts, block))
    code = own_ref[0:8, :].astype(jnp.int32) + 2 * LANES
    index, which = jnp.bitwise_and(code, LANES - 1), lax.shift_right_logical(code, 7)
    place = pick([lookup(places_of[r], index) for r in range(4)], which).astype(jnp.int32)
    own_place = own_ref[16:24, :].astype(jnp.int32)
    after = lax.shift_right_logical(place, 5) > lax.shift_right_logical(own_place, 5)
    late = jnp.where(after, own_ref[8:16, :], 0.0)
    starts = [pltpu.roll(meta[8:16] + meta[16:24], 32, 1) for meta in metas[:4]]
    held = None
    for i in range(8):
        at, owner = spread_row(place, i), spread_row(which, i)
        term = pick([lookup(start, at) for start in starts], owner) * spread_row(late, i)
        held = term if held is None else held + term
    names = own_ref[32:40, :].astype(jnp.int32)
    base = lookup(projected - held, names)
    gram = lookup(gram, names)
    gram_ref[...] = gram
    message = jnp.where(lane < QUARTER, jnp.maximum(base / gram, 0.0), base)
    listed = lookup(own_ref[8:16, :], names)
    rest = split2(listed)[1]
    spare = jnp.where(row < 4, spread_row(rest, LOW_SENT), spread_row(rest, LOW_SENT + 1))
    spare = jnp.where(row < 2, gram, spare)
    spare = jnp.where(jnp.bitwise_and(row, 1) == 0, pltpu.roll(spare, 64, 1), pltpu.roll(spare, 32, 1))
    others = jnp.where(lane < 96, message, spare)
    for t in range(n * tm):
        out_ref[t] = others
    for i, rel in enumerate(REACH):
        source = message if i == 0 else others
        turned = source if i % 4 == 0 else pltpu.roll(source, QUARTER * (i % 4), 1)
        target = tile_at(me, (-rel[0], rel[1]), n)
        for t in range(tm):
            out_ref[entry(message_slots, target * tm + t)] = turned
    codes = []
    for i in range(8):
        code = metas[i][0:8].astype(jnp.int32) + 2 * LANES
        at = [reach_at(REACH[i], near) for near in NEAR]
        device = pick(at, lax.shift_right_logical(code, 7))
        codes.append((device * LANES + jnp.bitwise_and(code, LANES - 1)).astype(jnp.float32))

    def gathered(parts, group, colour, start):
        out = None
        for q in range(4):
            p = (q + colour) % 4
            shift = (QUARTER * p - start) % LANES
            turned = parts[4 * group + q]
            turned = turned if shift == 0 else pltpu.roll(turned, shift, 1)
            out = turned if out is None else jnp.where(block == p, turned, out)
        return out

    high = [meta[0:8] for meta in metas[:8]]
    slot = 0
    for step, (group, colour) in enumerate(((0, 1), (1, 1), (0, 2), (0, 3))):
        if step < 3:
            start = QUARTER * (colour - 1)
            code = gathered(codes, group, colour, start).astype(jnp.int32)
            low = [jnp.where(row < LOW_SENT, meta[8 * colour : 8 * colour + 8], 0.0) for meta in metas[:8]]
            weight = gathered(high, group, colour, start + 64) + gathered(low, group, colour, 96)
            if group == 0:
                weight = jnp.where(block == colour, listed, weight)
            device, at = lax.shift_right_logical(code, 7), jnp.bitwise_and(code, LANES - 1)
            devices = range(12) if step == 1 else range(8)
        else:
            weight = listed
            device, at = lookup(which, names), lookup(index, names)
            devices = range(4)
        lanes, parts = edges(devices, places_of, device, at, weight, SOURCES[step])
        lanes_ref[8 * step : 8 * step + 8, :] = lanes
        for part in parts:
            weights_ref[8 * slot : 8 * slot + 8, :] = part
            slot += 1


def sweep_kernel(n, tm, message_slots, recv_ref, gram_ref, own_ref, lanes_ref, weights_ref, traces_ref, rms_ref):
    me = lax.axis_index("tile")
    half = lax.axis_index("tm")
    lane = iota((8, LANES), 1)
    block = lax.shift_right_logical(lane, 5)
    first = [tile_at(me, rel, n) * tm for rel in REACH]
    gram = gram_ref[...]

    def gathered(messages, group, turn):
        out = messages[4 * group]
        for q in range(4):
            if q or turn:
                out = jnp.where(block == (q + turn) % 4, messages[4 * group + q], out)
        return out

    def spare_of(messages, group, colour):
        return pltpu.roll(gathered(messages, group, 3), 64 if colour == 1 else 96, 1)

    def gram_of(spare, group, colour):
        rows = spread_row(spare, colour - 1)
        return jnp.where(block == colour, gram, rows) if group == 0 else rows

    def neighbours(step, tiles, spare, group, colour):
        slot = sum(len(sources) for sources in SOURCES[:step])
        total = None
        for i in range(8):
            at = jnp.broadcast_to(lanes_ref[8 * step + i : 8 * step + i + 1, :], (8, LANES))
            for s, tile in enumerate(tiles):
                place = 8 * (slot + s) + i
                weight = jnp.broadcast_to(weights_ref[place : place + 1, :], (8, LANES))
                if spare is not None and i >= LOW_SENT:
                    low = spread_row(spare, 2 * (i - LOW_SENT) + 1 + colour)
                    low = jnp.where(block == colour, 0.0, low) if group == 0 else low
                    weight = jnp.where(weight != 0.0, weight + low, 0.0)
                term = lookup(tile, at) * weight
                total = term if total is None else total + term
        return total

    energy, mine = None, None
    for t in range(tm):
        messages = [recv_ref[entry(message_slots, f + t)] for f in first]
        x0 = [gathered(messages, group, 0) for group in range(3)]
        x1 = []
        for group in range(2):
            spare = spare_of(messages, group, 1)
            fresh = gathered(messages, group, 1) - neighbours(group, x0[: 2 + group], spare, group, 1)
            x1.append(jnp.maximum(fresh / gram_of(spare, group, 1), 0.0))
        spare = spare_of(messages, 0, 2)
        fresh = gathered(messages, 0, 2) - neighbours(2, [x0[0], x0[1], x1[0], x1[1]], spare, 0, 2)
        x2 = jnp.maximum(fresh / gram_of(spare, 0, 2), 0.0)
        fresh = messages[0] - neighbours(3, [x0[0], x1[0], x2], None, 0, 3)
        x3 = jnp.maximum(fresh / gram, 0.0)
        own = pick([messages[0], x1[0], x2, x3], block)
        square = jnp.sum(own * own, axis=0, keepdims=True)
        energy = square if energy is None else energy + square
        mine = own if mine is None else jnp.where(half == t, own, mine)
    order = own_ref[16:24, :].astype(jnp.int32)
    traces_ref[...] = lookup(mine, order)
    energy = lookup(jnp.broadcast_to(energy, (8, LANES)), order)
    rms_ref[...] = jnp.sqrt(energy[0:1] / (8 * tm) + 1e-06)


def shards(
    data, send_list, footprint_slot, footprint, colour, correlation, correlation_gram, traces_init
):
    n = lax.axis_size("tile")
    tm = lax.axis_size("tm")
    tiles, devices = ORDERS.get((n, tm), (list(range(n)), list(range(n * tm))))
    f32, bf16 = jnp.float32, jnp.bfloat16
    shape = jax.ShapeDtypeStruct
    vmem = pl.BlockSpec(memory_space=pltpu.VMEM)
    hbm = pl.BlockSpec(memory_space=pltpu.HBM)

    def call(body, outs, ins, scratch=(), limit=VMEM_LIMIT):
        return pl.pallas_call(
            body,
            out_shape=outs,
            in_specs=ins,
            out_specs=[vmem] * len(outs),
            scratch_shapes=scratch,
            compiler_params=pltpu.CompilerParams(vmem_limit_bytes=limit),
        )

    inputs = (
        colour.reshape(1, LANES), correlation.T, correlation_gram.T, traces_init, footprint_slot.T,
        send_list[0].T, data,
    )
    outgoing, own = call(
        functools.partial(pack_kernel, n, slots_of(tiles)),
        [shape((n, DATA_ROWS + META_ROWS, LANES), bf16), shape((40, LANES), f32)],
        [hbm] * 7,
        [pltpu.VMEM(x.shape, x.dtype) for x in inputs[:5]]
        + [pltpu.SMEM(inputs[5].shape, jnp.int32), pltpu.VMEM(data.shape, bf16)]
        + [pltpu.SemaphoreType.DMA((7,))],
        PACK_LIMIT,
    )(*[pltpu.with_memory_space_constraint(x, pltpu.HBM) for x in inputs])
    arrived = lax.all_to_all(
        outgoing, "tile", split_axis=0, concat_axis=0, tiled=True, axis_index_groups=[tiles]
    )
    slots = sum(len(sources) for sources in SOURCES)
    message, gram, lanes, weights = call(
        functools.partial(project_kernel, n, tm, slots_of(tiles), slots_of(devices)),
        [shape((n * tm, 8, LANES), f32), shape((8, LANES), f32)]
        + [shape((8 * len(SOURCES), LANES), jnp.int32), shape((8 * slots, LANES), f32)],
        [vmem] * 3,
        [pltpu.VMEM((8 * LANES, LANES), f32)],
    )(arrived, footprint.reshape(8 * LANES, LANES), own)
    messages = lax.all_to_all(
        message, ("tile", "tm"), split_axis=0, concat_axis=0, tiled=True, axis_index_groups=[devices]
    )
    traces, rms = call(
        functools.partial(sweep_kernel, n, tm, slots_of(devices)),
        [shape((8, LANES), f32), shape((1, LANES), f32)],
        [vmem] * 5,
    )(messages, gram, own, lanes, weights)
    return (traces, rms.reshape(LANES))


def solution(mesh):
    placed = (
        P("tile", "tm", None),
        P("tile", None, None),
        P("tile", None),
        P("tile", None, None),
        P("tile"),
        P("tile", None),
        P("tile", None),
        P("tm", "tile"),
    )
    return jax.shard_map(
        shards, mesh=mesh, in_specs=placed, out_specs=(P("tm", "tile"), P("tile")), check_vma=False
    )
```

```python
import functools

import jax
import jax.numpy as jnp
from jax import lax
from jax.experimental import pallas as pl
from jax.experimental.pallas import tpu as pltpu
from jax.sharding import PartitionSpec as P

REACH = (
    (0, 0), (1, 0), (-1, 0), (0, 1),
    (1, 1), (-1, 1), (2, 0), (-2, 0),
    (3, 0), (-3, 0), (2, 1), (-2, 1),
)
NEAR = REACH[:4]
ORDERS = {
    (16, 2): (
        [5, 1, 4, 10, 9, 15, 14, 12, 3, 2, 11, 8, 6, 7, 13, 0],
        [0, 17, 26, 21, 1, 25, 7, 24, 29, 9, 16, 5, 22, 12, 18, 8]
        + [13, 20, 28, 14, 19, 3, 2, 4, 23, 31, 27, 10, 6, 11, 15, 30],
    ),
}
LANES = 128
QUARTER = 32
DATA_ROWS = 64
META_ROWS = 24
LOW_SENT = 6
GROUP = 4
VMEM_LIMIT = 48 * 2 ** 20
PACK_LIMIT = 48 * 2 ** 20
NT = (((1,), (1,)), ((), ()))


def iota(shape, dim):
    return lax.broadcasted_iota(jnp.int32, shape, dim)


def reach_at(device, near):
    return REACH.index((device[0] + near[0], (device[1] + near[1]) % 2))


def tile_at(me, rel, n):
    return lax.rem(me + rel[0] + rel[1] * (n // 2) + n, n)


def slots_of(order):
    return [order.index(device) for device in range(len(order))]


def entry(table, i):
    if table == list(range(len(table))):
        return i
    words = [sum(table[w + b] << (8 * b) for b in range(4)) for w in range(0, len(table), 4)]
    word, at = words[0], lax.shift_right_logical(i, 2)
    for w in range(1, len(words)):
        word = jnp.where(at == w, words[w], word)
    return jnp.bitwise_and(lax.shift_right_logical(word, 8 * jnp.bitwise_and(i, 3)), 255)


def dot(a, b):
    return jnp.dot(a, b, preferred_element_type=jnp.float32)


def dot_nt(a, b):
    return lax.dot_general(a, b, NT, preferred_element_type=jnp.float32)


def split2(x):
    hi = x.astype(jnp.bfloat16).astype(jnp.float32)
    return hi, x - hi


def split3(x):
    hi, rest = split2(x)
    mid, low = split2(rest)
    return jnp.concatenate([hi, mid, low], axis=0).astype(jnp.bfloat16)


def places(colour_row):
    in_class = colour_row == iota((8, LANES), 0)
    before = (iota((LANES, LANES), 0) < iota((LANES, LANES), 1)).astype(jnp.bfloat16)
    counts = dot(in_class.astype(jnp.bfloat16), before)
    rank = jnp.sum(jnp.where(in_class, counts, 0.0), axis=0, keepdims=True)
    return rank + (colour_row * QUARTER).astype(jnp.float32)


def pack_kernel(n, slots, *refs):
    sources, (out_ref, own_ref), held, sems = refs[:7], refs[7:9], refs[9:16], refs[16]
    colour_ref, corr_ref, gram_ref, init_ref, slot_ref, send_ref, data_ref = held
    copies = [pltpu.make_async_copy(a, b, sems.at[i]) for i, (a, b) in enumerate(zip(sources, held))]
    for copy in copies:
        copy.start()
    me = lax.axis_index("tile")
    lane = iota((8, LANES), 1)
    row = iota((8, LANES), 0)
    for copy in copies[:5]:
        copy.wait()
    own_ref[24:32, :] = slot_ref[...].astype(jnp.float32)
    pos = places(colour_ref[...])
    order = (iota((LANES, LANES), 0).astype(jnp.float32) == pos).astype(jnp.bfloat16)
    ids = corr_ref[...]
    away = jnp.bitwise_and(lax.shift_right_logical(ids, 7) - me, n - 1)
    which = jnp.where(away == 0, 0, jnp.where(away == 1, 1, jnp.where(away == n - 1, 2, 3)))
    code = which * LANES + jnp.bitwise_and(ids, LANES - 1) - 2 * LANES
    code = code.astype(jnp.float32)
    gram = gram_ref[...]
    gram_hi, gram_lo = split2(gram)
    init_hi, init_lo = split2(init_ref[...])
    rows = [code, gram_hi, gram_lo, init_hi, init_lo, lane.astype(jnp.float32)]
    placed = dot_nt(jnp.concatenate(rows, axis=0).astype(jnp.bfloat16), order)
    placed = [placed[8 * i : 8 * i + 8] for i in range(6)]
    pos = jnp.broadcast_to(pos, (8, LANES))
    own_ref[0:8, :] = code
    own_ref[8:16, :] = gram
    own_ref[16:24, :] = pos
    own_ref[32:40, :] = placed[5]
    first = jnp.where(lane < 64, pltpu.roll(placed[0], 96, 1), pltpu.roll(placed[1], 32, 1))
    tails = []
    for low, even, odd in ((64, 96, 64), (32, 32, 0)):
        even = pltpu.roll(pos, even, 1)
        odd = pltpu.roll(pos, odd, 1) if odd else pos
        tails.append(
            jnp.where(row < LOW_SENT, pltpu.roll(placed[2], low, 1), jnp.where(row == LOW_SENT, even, odd))
        )
    second = jnp.where(lane < 96, pltpu.roll(placed[3], 96, 1), tails[0])
    third = jnp.where(lane < 96, pltpu.roll(placed[4], 96, 1), tails[1])
    meta = jnp.concatenate([first, second, third], axis=0)
    for copy in copies[5:]:
        copy.wait()
    for target in range(n):
        blocks = [data_ref[send_ref[c, target]].astype(jnp.float32) for c in range(8)]
        out_ref[slots[target]] = jnp.concatenate(blocks + [meta], axis=0).astype(jnp.bfloat16)


def column(row):
    eye = iota((LANES, LANES), 0) == iota((LANES, LANES), 1)
    return dot(jnp.where(eye, row, 0.0).astype(jnp.bfloat16), jnp.ones((LANES, LANES), jnp.bfloat16))


def lookup(table, index):
    return jnp.take_along_axis(table, index, axis=1, mode="promise_in_bounds")


def spread_row(rows, i):
    return jnp.broadcast_to(rows[i : i + 1], (8, LANES))


def pick(cases, which):
    out = cases[-1]
    for i in range(len(cases) - 1):
        out = jnp.where(which == i, cases[i], out)
    return out


def edges(devices, places_of, which, index, weight, sources):
    place, device = None, None
    for f in devices:
        found = lookup(places_of[f], index)
        place = found if place is None else jnp.where(which == f, found, place)
    place = place.astype(jnp.int32)
    colour = lax.shift_right_logical(place, 5)
    turn = jnp.bitwise_and(which + colour, 3)
    lanes = turn * QUARTER + jnp.bitwise_and(place, QUARTER - 1)
    tile = colour * 4 + lax.shift_right_logical(which, 2)
    return lanes, [jnp.where(tile == c * 4 + g, weight, 0.0) for c, g in sources]


SOURCES = (
    ((0, 0), (0, 1)),
    ((0, 0), (0, 1), (0, 2)),
    ((0, 0), (0, 1), (1, 0), (1, 1)),
    ((0, 0), (1, 0), (2, 0)),
)


def project_kernel(n, tm, slots, message_slots, recv_ref, fp_ref, own_ref, out_ref, gram_ref, lanes_ref, weights_ref, wide_ref):
    me = lax.axis_index("tile")
    lane = iota((8, LANES), 1)
    row = iota((8, LANES), 0)
    wide_ref[...] = fp_ref[...].astype(jnp.float32)
    weights, squares = [], None
    cut = 4 * n
    upper = (own_ref[24:32, :] >= float(cut)).astype(jnp.float32)
    for j in range(8):
        rows = wide_ref[pl.ds(j, LANES, stride=8), :]
        squares = rows * rows if j == 0 else squares + rows * rows
        above = column(upper[j : j + 1]) * rows
        weights.append(jnp.concatenate([rows - above, above], axis=1).astype(jnp.bfloat16))
    weights = jnp.concatenate(weights, axis=0)
    gram = dot_nt(jnp.ones((8, LANES), jnp.bfloat16), split3(squares))
    gram = gram[:, :LANES] + gram[:, LANES : 2 * LANES] + gram[:, 2 * LANES :]
    slot_rows = own_ref[24:32, :] - upper * float(cut)
    slot_row = jnp.concatenate([slot_rows[j : j + 1] for j in range(8)], axis=1)
    slot_row = jnp.broadcast_to(slot_row, (8, 8 * LANES))
    total = jnp.zeros((8, 8 * LANES), jnp.float32)
    for source in range(0, n // 2, GROUP):
        halves = []
        for first in (source, source + n // 2):
            blocks = [recv_ref[slots[first + i], :DATA_ROWS, :] for i in range(GROUP)]
            halves.append(jnp.concatenate(blocks, axis=0))
        product = dot_nt(jnp.concatenate(halves, axis=1), weights)
        for c in range(GROUP * 8):
            hit = slot_row == float(source * 8 + c)
            total = jnp.where(hit, product[8 * c : 8 * c + 8], total)
    projected = total[:, :LANES]
    for j in range(1, 8):
        projected = projected + total[:, j * LANES : (j + 1) * LANES]
    block = lax.shift_right_logical(lane, 5)
    metas = [recv_ref[entry(slots, tile_at(me, rel, n))].astype(jnp.float32)[DATA_ROWS:] for rel in REACH]
    places_of = []
    for meta in metas:
        parts = [spread_row(meta, 8 + LOW_SENT), spread_row(meta, 9 + LOW_SENT)]
        parts += [spread_row(meta, 16 + LOW_SENT), spread_row(meta, 17 + LOW_SENT)]
        parts = [pltpu.roll(part, 32 * i + 32, 1) if i < 3 else part for i, part in enumerate(parts)]
        places_of.append(pick(parts, block))
    code = own_ref[0:8, :].astype(jnp.int32) + 2 * LANES
    index, which = jnp.bitwise_and(code, LANES - 1), lax.shift_right_logical(code, 7)
    place = pick([lookup(places_of[r], index) for r in range(4)], which).astype(jnp.int32)
    own_place = own_ref[16:24, :].astype(jnp.int32)
    after = lax.shift_right_logical(place, 5) > lax.shift_right_logical(own_place, 5)
    late = jnp.where(after, own_ref[8:16, :], 0.0)
    starts = [pltpu.roll(meta[8:16] + meta[16:24], 32, 1) for meta in metas[:4]]
    held = None
    for i in range(8):
        at, owner = spread_row(place, i), spread_row(which, i)
        term = pick([lookup(start, at) for start in starts], owner) * spread_row(late, i)
        held = term if held is None else held + term
    names = own_ref[32:40, :].astype(jnp.int32)
    base = lookup(projected - held, names)
    gram = lookup(gram, names)
    gram_ref[...] = gram
    message = jnp.where(lane < QUARTER, jnp.maximum(base / gram, 0.0), base)
    listed = lookup(own_ref[8:16, :], names)
    rest = split2(listed)[1]
    spare = jnp.where(row < 4, spread_row(rest, LOW_SENT), spread_row(rest, LOW_SENT + 1))
    spare = jnp.where(row < 2, gram, spare)
    spare = jnp.where(jnp.bitwise_and(row, 1) == 0, pltpu.roll(spare, 64, 1), pltpu.roll(spare, 32, 1))
    others = jnp.where(lane < 96, message, spare)
    for t in range(n * tm):
        out_ref[t] = others
    for i, rel in enumerate(REACH):
        source = message if i == 0 else others
        turned = source if i % 4 == 0 else pltpu.roll(source, QUARTER * (i % 4), 1)
        target = tile_at(me, (-rel[0], rel[1]), n)
        for t in range(tm):
            out_ref[entry(message_slots, target * tm + t)] = turned
    codes = []
    for i in range(8):
        code = metas[i][0:8].astype(jnp.int32) + 2 * LANES
        at = [reach_at(REACH[i], near) for near in NEAR]
        device = pick(at, lax.shift_right_logical(code, 7))
        codes.append((device * LANES + jnp.bitwise_and(code, LANES - 1)).astype(jnp.float32))

    def gathered(parts, group, colour, start):
        out = None
        for q in range(4):
            p = (q + colour) % 4
            shift = (QUARTER * p - start) % LANES
            turned = parts[4 * group + q]
            turned = turned if shift == 0 else pltpu.roll(turned, shift, 1)
            out = turned if out is None else jnp.where(block == p, turned, out)
        return out

    high = [meta[0:8] for meta in metas[:8]]
    slot = 0
    for step, (group, colour) in enumerate(((0, 1), (1, 1), (0, 2), (0, 3))):
        if step < 3:
            start = QUARTER * (colour - 1)
            code = gathered(codes, group, colour, start).astype(jnp.int32)
            low = [jnp.where(row < LOW_SENT, meta[8 * colour : 8 * colour + 8], 0.0) for meta in metas[:8]]
            weight = gathered(high, group, colour, start + 64) + gathered(low, group, colour, 96)
            if group == 0:
                weight = jnp.where(block == colour, listed, weight)
            device, at = lax.shift_right_logical(code, 7), jnp.bitwise_and(code, LANES - 1)
            devices = range(12) if step == 1 else range(8)
        else:
            weight = listed
            device, at = lookup(which, names), lookup(index, names)
            devices = range(4)
        lanes, parts = edges(devices, places_of, device, at, weight, SOURCES[step])
        lanes_ref[8 * step : 8 * step + 8, :] = lanes
        for part in parts:
            weights_ref[8 * slot : 8 * slot + 8, :] = part
            slot += 1


def sweep_kernel(n, tm, message_slots, recv_ref, gram_ref, own_ref, lanes_ref, weights_ref, traces_ref, rms_ref):
    me = lax.axis_index("tile")
    half = lax.axis_index("tm")
    lane = iota((8, LANES), 1)
    block = lax.shift_right_logical(lane, 5)
    first = [tile_at(me, rel, n) * tm for rel in REACH]
    gram = gram_ref[...]

    def gathered(messages, group, turn):
        out = messages[4 * group]
        for q in range(4):
            if q or turn:
                out = jnp.where(block == (q + turn) % 4, messages[4 * group + q], out)
        return out

    def spare_of(messages, group, colour):
        return pltpu.roll(gathered(messages, group, 3), 64 if colour == 1 else 96, 1)

    def gram_of(spare, group, colour):
        rows = spread_row(spare, colour - 1)
        return jnp.where(block == colour, gram, rows) if group == 0 else rows

    def neighbours(step, tiles, spare, group, colour):
        slot = sum(len(sources) for sources in SOURCES[:step])
        total = None
        for i in range(8):
            at = jnp.broadcast_to(lanes_ref[8 * step + i : 8 * step + i + 1, :], (8, LANES))
            for s, tile in enumerate(tiles):
                place = 8 * (slot + s) + i
                weight = jnp.broadcast_to(weights_ref[place : place + 1, :], (8, LANES))
                if spare is not None and i >= LOW_SENT:
                    low = spread_row(spare, 2 * (i - LOW_SENT) + 1 + colour)
                    low = jnp.where(block == colour, 0.0, low) if group == 0 else low
                    weight = jnp.where(weight != 0.0, weight + low, 0.0)
                term = lookup(tile, at) * weight
                total = term if total is None else total + term
        return total

    energy, mine = None, None
    for t in range(tm):
        messages = [recv_ref[entry(message_slots, f + t)] for f in first]
        x0 = [gathered(messages, group, 0) for group in range(3)]
        x1 = []
        for group in range(2):
            spare = spare_of(messages, group, 1)
            fresh = gathered(messages, group, 1) - neighbours(group, x0[: 2 + group], spare, group, 1)
            x1.append(jnp.maximum(fresh / gram_of(spare, group, 1), 0.0))
        spare = spare_of(messages, 0, 2)
        fresh = gathered(messages, 0, 2) - neighbours(2, [x0[0], x0[1], x1[0], x1[1]], spare, 0, 2)
        x2 = jnp.maximum(fresh / gram_of(spare, 0, 2), 0.0)
        fresh = messages[0] - neighbours(3, [x0[0], x1[0], x2], None, 0, 3)
        x3 = jnp.maximum(fresh / gram, 0.0)
        own = pick([messages[0], x1[0], x2, x3], block)
        square = jnp.sum(own * own, axis=0, keepdims=True)
        energy = square if energy is None else energy + square
        mine = own if mine is None else jnp.where(half == t, own, mine)
    order = own_ref[16:24, :].astype(jnp.int32)
    traces_ref[...] = lookup(mine, order)
    energy = lookup(jnp.broadcast_to(energy, (8, LANES)), order)
    rms_ref[...] = jnp.sqrt(energy[0:1] / (8 * tm) + 1e-06)


def shards(
    data, send_list, footprint_slot, footprint, colour, correlation, correlation_gram, traces_init
):
    n = lax.axis_size("tile")
    tm = lax.axis_size("tm")
    tiles, devices = ORDERS.get((n, tm), (list(range(n)), list(range(n * tm))))
    f32, bf16 = jnp.float32, jnp.bfloat16
    shape = jax.ShapeDtypeStruct
    vmem = pl.BlockSpec(memory_space=pltpu.VMEM)
    hbm = pl.BlockSpec(memory_space=pltpu.HBM)

    def call(body, outs, ins, scratch=(), limit=VMEM_LIMIT):
        return pl.pallas_call(
            body,
            out_shape=outs,
            in_specs=ins,
            out_specs=[vmem] * len(outs),
            scratch_shapes=scratch,
            compiler_params=pltpu.CompilerParams(vmem_limit_bytes=limit),
        )

    inputs = (
        colour.reshape(1, LANES), correlation.T, correlation_gram.T, traces_init, footprint_slot.T,
        send_list[0].T, data,
    )
    outgoing, own = call(
        functools.partial(pack_kernel, n, slots_of(tiles)),
        [shape((n, DATA_ROWS + META_ROWS, LANES), bf16), shape((40, LANES), f32)],
        [hbm] * 7,
        [pltpu.VMEM(x.shape, x.dtype) for x in inputs[:5]]
        + [pltpu.SMEM(inputs[5].shape, jnp.int32), pltpu.VMEM(data.shape, bf16)]
        + [pltpu.SemaphoreType.DMA((7,))],
        PACK_LIMIT,
    )(*[pltpu.with_memory_space_constraint(x, pltpu.HBM) for x in inputs])
    arrived = lax.all_to_all(
        outgoing, "tile", split_axis=0, concat_axis=0, tiled=True, axis_index_groups=[tiles]
    )
    slots = sum(len(sources) for sources in SOURCES)
    message, gram, lanes, weights = call(
        functools.partial(project_kernel, n, tm, slots_of(tiles), slots_of(devices)),
        [shape((n * tm, 8, LANES), f32), shape((8, LANES), f32)]
        + [shape((8 * len(SOURCES), LANES), jnp.int32), shape((8 * slots, LANES), f32)],
        [vmem] * 3,
        [pltpu.VMEM((8 * LANES, LANES), f32)],
    )(arrived, footprint.reshape(8 * LANES, LANES), own)
    messages = lax.all_to_all(
        message, ("tile", "tm"), split_axis=0, concat_axis=0, tiled=True, axis_index_groups=[devices]
    )
    traces, rms = call(
        functools.partial(sweep_kernel, n, tm, slots_of(devices)),
        [shape((8, LANES), f32), shape((1, LANES), f32)],
        [vmem] * 5,
    )(messages, gram, own, lanes, weights)
    return (traces, rms.reshape(LANES))


def solution(mesh):
    placed = (
        P("tile", "tm", None),
        P("tile", None, None),
        P("tile", None),
        P("tile", None, None),
        P("tile"),
        P("tile", None),
        P("tile", None),
        P("tm", "tile"),
    )
    return jax.shard_map(
        shards, mesh=mesh, in_specs=placed, out_specs=(P("tm", "tile"), P("tile")), check_vma=False
    )
```

```python
import functools

import jax
import jax.numpy as jnp
from jax import lax
from jax.experimental import pallas as pl
from jax.experimental.pallas import tpu as pltpu
from jax.sharding import PartitionSpec as P

REACH = (
    (0, 0), (1, 0), (-1, 0), (0, 1),
    (1, 1), (-1, 1), (2, 0), (-2, 0),
    (3, 0), (-3, 0), (2, 1), (-2, 1),
)
NEAR = REACH[:4]
ORDERS = {
    (16, 2): (
        [6, 4, 5, 0, 9, 15, 13, 3, 10, 2, 1, 12, 7, 14, 11, 8],
        [0, 17, 26, 21, 1, 25, 7, 24, 29, 9, 16, 5, 22, 12, 18, 8]
        + [13, 20, 28, 14, 19, 3, 2, 4, 23, 31, 27, 10, 6, 11, 15, 30],
    ),
}
LANES = 128
QUARTER = 32
DATA_ROWS = 64
META_ROWS = 24
LOW_SENT = 6
GROUP = 4
VMEM_LIMIT = 48 * 2 ** 20
PACK_LIMIT = 48 * 2 ** 20
NT = (((1,), (1,)), ((), ()))


def iota(shape, dim):
    return lax.broadcasted_iota(jnp.int32, shape, dim)


def reach_at(device, near):
    return REACH.index((device[0] + near[0], (device[1] + near[1]) % 2))


def tile_at(me, rel, n):
    return lax.rem(me + rel[0] + rel[1] * (n // 2) + n, n)


def slots_of(order):
    return [order.index(device) for device in range(len(order))]


def entry(table, i):
    if table == list(range(len(table))):
        return i
    words = [sum(table[w + b] << (8 * b) for b in range(4)) for w in range(0, len(table), 4)]
    word, at = words[0], lax.shift_right_logical(i, 2)
    for w in range(1, len(words)):
        word = jnp.where(at == w, words[w], word)
    return jnp.bitwise_and(lax.shift_right_logical(word, 8 * jnp.bitwise_and(i, 3)), 255)


def dot(a, b):
    return jnp.dot(a, b, preferred_element_type=jnp.float32)


def dot_nt(a, b):
    return lax.dot_general(a, b, NT, preferred_element_type=jnp.float32)


def split2(x):
    hi = x.astype(jnp.bfloat16).astype(jnp.float32)
    return hi, x - hi


def split3(x):
    hi, rest = split2(x)
    mid, low = split2(rest)
    return jnp.concatenate([hi, mid, low], axis=0).astype(jnp.bfloat16)


def places(colour_row):
    in_class = colour_row == iota((8, LANES), 0)
    before = (iota((LANES, LANES), 0) < iota((LANES, LANES), 1)).astype(jnp.bfloat16)
    counts = dot(in_class.astype(jnp.bfloat16), before)
    rank = jnp.sum(jnp.where(in_class, counts, 0.0), axis=0, keepdims=True)
    return rank + (colour_row * QUARTER).astype(jnp.float32)


def pack_kernel(n, slots, *refs):
    sources, (out_ref, own_ref), held, sems = refs[:7], refs[7:9], refs[9:16], refs[16]
    colour_ref, corr_ref, gram_ref, init_ref, slot_ref, send_ref, data_ref = held
    copies = [pltpu.make_async_copy(a, b, sems.at[i]) for i, (a, b) in enumerate(zip(sources, held))]
    for copy in copies:
        copy.start()
    me = lax.axis_index("tile")
    lane = iota((8, LANES), 1)
    row = iota((8, LANES), 0)
    copies[0].wait()
    pos = places(colour_ref[...])
    order = (iota((LANES, LANES), 0).astype(jnp.float32) == pos).astype(jnp.bfloat16)
    for copy in copies[1:5]:
        copy.wait()
    own_ref[24:32, :] = slot_ref[...].astype(jnp.float32)
    ids = corr_ref[...]
    away = jnp.bitwise_and(lax.shift_right_logical(ids, 7) - me, n - 1)
    which = jnp.where(away == 0, 0, jnp.where(away == 1, 1, jnp.where(away == n - 1, 2, 3)))
    code = which * LANES + jnp.bitwise_and(ids, LANES - 1) - 2 * LANES
    code = code.astype(jnp.float32)
    gram = gram_ref[...]
    gram_hi, gram_lo = split2(gram)
    init_hi, init_lo = split2(init_ref[...])
    rows = [code, gram_hi, gram_lo, init_hi, init_lo, lane.astype(jnp.float32)]
    placed = dot_nt(jnp.concatenate(rows, axis=0).astype(jnp.bfloat16), order)
    placed = [placed[8 * i : 8 * i + 8] for i in range(6)]
    pos = jnp.broadcast_to(pos, (8, LANES))
    own_ref[0:8, :] = code
    own_ref[8:16, :] = gram
    own_ref[16:24, :] = pos
    own_ref[32:40, :] = placed[5]
    first = jnp.where(lane < 64, pltpu.roll(placed[0], 96, 1), pltpu.roll(placed[1], 32, 1))
    tails = []
    for low, even, odd in ((64, 96, 64), (32, 32, 0)):
        even = pltpu.roll(pos, even, 1)
        odd = pltpu.roll(pos, odd, 1) if odd else pos
        tails.append(
            jnp.where(row < LOW_SENT, pltpu.roll(placed[2], low, 1), jnp.where(row == LOW_SENT, even, odd))
        )
    second = jnp.where(lane < 96, pltpu.roll(placed[3], 96, 1), tails[0])
    third = jnp.where(lane < 96, pltpu.roll(placed[4], 96, 1), tails[1])
    meta = jnp.concatenate([first, second, third], axis=0)
    for copy in copies[5:]:
        copy.wait()
    for target in range(n):
        blocks = [data_ref[send_ref[c, target]].astype(jnp.float32) for c in range(8)]
        out_ref[slots[target]] = jnp.concatenate(blocks + [meta], axis=0).astype(jnp.bfloat16)


def column(row):
    eye = iota((LANES, LANES), 0) == iota((LANES, LANES), 1)
    return dot(jnp.where(eye, row, 0.0).astype(jnp.bfloat16), jnp.ones((LANES, LANES), jnp.bfloat16))


def lookup(table, index):
    return jnp.take_along_axis(table, index, axis=1, mode="promise_in_bounds")


def spread_row(rows, i):
    return jnp.broadcast_to(rows[i : i + 1], (8, LANES))


def pick(cases, which):
    out = cases[-1]
    for i in range(len(cases) - 1):
        out = jnp.where(which == i, cases[i], out)
    return out


def edges(devices, places_of, which, index, weight, sources):
    place, device = None, None
    for f in devices:
        found = lookup(places_of[f], index)
        place = found if place is None else jnp.where(which == f, found, place)
    place = place.astype(jnp.int32)
    colour = lax.shift_right_logical(place, 5)
    turn = jnp.bitwise_and(which + colour, 3)
    lanes = turn * QUARTER + jnp.bitwise_and(place, QUARTER - 1)
    tile = colour * 4 + lax.shift_right_logical(which, 2)
    return lanes, [jnp.where(tile == c * 4 + g, weight, 0.0) for c, g in sources]


SOURCES = (
    ((0, 0), (0, 1)),
    ((0, 0), (0, 1), (0, 2)),
    ((0, 0), (0, 1), (1, 0), (1, 1)),
    ((0, 0), (1, 0), (2, 0)),
)


def project_kernel(n, tm, slots, message_slots, recv_ref, fp_ref, own_ref, out_ref, gram_ref, lanes_ref, weights_ref, wide_ref):
    me = lax.axis_index("tile")
    lane = iota((8, LANES), 1)
    row = iota((8, LANES), 0)
    wide_ref[...] = fp_ref[...].astype(jnp.float32)
    weights, squares = [], None
    cut = 4 * n
    upper = (own_ref[24:32, :] >= float(cut)).astype(jnp.float32)
    for j in range(8):
        rows = wide_ref[pl.ds(j, LANES, stride=8), :]
        squares = rows * rows if j == 0 else squares + rows * rows
        above = column(upper[j : j + 1]) * rows
        weights.append(jnp.concatenate([rows - above, above], axis=1).astype(jnp.bfloat16))
    weights = jnp.concatenate(weights, axis=0)
    gram = dot_nt(jnp.ones((8, LANES), jnp.bfloat16), split3(squares))
    gram = gram[:, :LANES] + gram[:, LANES : 2 * LANES] + gram[:, 2 * LANES :]
    slot_rows = own_ref[24:32, :] - upper * float(cut)
    slot_row = jnp.concatenate([slot_rows[j : j + 1] for j in range(8)], axis=1)
    slot_row = jnp.broadcast_to(slot_row, (8, 8 * LANES))
    total = jnp.zeros((8, 8 * LANES), jnp.float32)
    for source in range(0, n // 2, GROUP):
        halves = []
        for first in (source, source + n // 2):
            blocks = [recv_ref[slots[first + i], :DATA_ROWS, :] for i in range(GROUP)]
            halves.append(jnp.concatenate(blocks, axis=0))
        product = dot_nt(jnp.concatenate(halves, axis=1), weights)
        for c in range(GROUP * 8):
            hit = slot_row == float(source * 8 + c)
            total = jnp.where(hit, product[8 * c : 8 * c + 8], total)
    projected = total[:, :LANES]
    for j in range(1, 8):
        projected = projected + total[:, j * LANES : (j + 1) * LANES]
    block = lax.shift_right_logical(lane, 5)
    metas = [recv_ref[entry(slots, tile_at(me, rel, n))].astype(jnp.float32)[DATA_ROWS:] for rel in REACH]
    places_of = []
    for meta in metas:
        parts = [spread_row(meta, 8 + LOW_SENT), spread_row(meta, 9 + LOW_SENT)]
        parts += [spread_row(meta, 16 + LOW_SENT), spread_row(meta, 17 + LOW_SENT)]
        parts = [pltpu.roll(part, 32 * i + 32, 1) if i < 3 else part for i, part in enumerate(parts)]
        places_of.append(pick(parts, block))
    code = own_ref[0:8, :].astype(jnp.int32) + 2 * LANES
    index, which = jnp.bitwise_and(code, LANES - 1), lax.shift_right_logical(code, 7)
    place = pick([lookup(places_of[r], index) for r in range(4)], which).astype(jnp.int32)
    own_place = own_ref[16:24, :].astype(jnp.int32)
    after = lax.shift_right_logical(place, 5) > lax.shift_right_logical(own_place, 5)
    late = jnp.where(after, own_ref[8:16, :], 0.0)
    starts = [pltpu.roll(meta[8:16] + meta[16:24], 32, 1) for meta in metas[:4]]
    held = None
    for i in range(8):
        at, owner = spread_row(place, i), spread_row(which, i)
        term = pick([lookup(start, at) for start in starts], owner) * spread_row(late, i)
        held = term if held is None else held + term
    names = own_ref[32:40, :].astype(jnp.int32)
    base = lookup(projected - held, names)
    gram = lookup(gram, names)
    gram_ref[...] = gram
    message = jnp.where(lane < QUARTER, jnp.maximum(base / gram, 0.0), base)
    listed = lookup(own_ref[8:16, :], names)
    rest = split2(listed)[1]
    spare = jnp.where(row < 4, spread_row(rest, LOW_SENT), spread_row(rest, LOW_SENT + 1))
    spare = jnp.where(row < 2, gram, spare)
    spare = jnp.where(jnp.bitwise_and(row, 1) == 0, pltpu.roll(spare, 64, 1), pltpu.roll(spare, 32, 1))
    others = jnp.where(lane < 96, message, spare)
    for t in range(n * tm):
        out_ref[t] = others
    for i, rel in enumerate(REACH):
        source = message if i == 0 else others
        turned = source if i % 4 == 0 else pltpu.roll(source, QUARTER * (i % 4), 1)
        target = tile_at(me, (-rel[0], rel[1]), n)
        for t in range(tm):
            out_ref[entry(message_slots, target * tm + t)] = turned
    codes = []
    for i in range(8):
        code = metas[i][0:8].astype(jnp.int32) + 2 * LANES
        at = [reach_at(REACH[i], near) for near in NEAR]
        device = pick(at, lax.shift_right_logical(code, 7))
        codes.append((device * LANES + jnp.bitwise_and(code, LANES - 1)).astype(jnp.float32))

    def gathered(parts, group, colour, start):
        out = None
        for q in range(4):
            p = (q + colour) % 4
            shift = (QUARTER * p - start) % LANES
            turned = parts[4 * group + q]
            turned = turned if shift == 0 else pltpu.roll(turned, shift, 1)
            out = turned if out is None else jnp.where(block == p, turned, out)
        return out

    high = [meta[0:8] for meta in metas[:8]]
    slot = 0
    for step, (group, colour) in enumerate(((0, 1), (1, 1), (0, 2), (0, 3))):
        if step < 3:
            start = QUARTER * (colour - 1)
            code = gathered(codes, group, colour, start).astype(jnp.int32)
            low = [jnp.where(row < LOW_SENT, meta[8 * colour : 8 * colour + 8], 0.0) for meta in metas[:8]]
            weight = gathered(high, group, colour, start + 64) + gathered(low, group, colour, 96)
            if group == 0:
                weight = jnp.where(block == colour, listed, weight)
            device, at = lax.shift_right_logical(code, 7), jnp.bitwise_and(code, LANES - 1)
            devices = range(12) if step == 1 else range(8)
        else:
            weight = listed
            device, at = lookup(which, names), lookup(index, names)
            devices = range(4)
        lanes, parts = edges(devices, places_of, device, at, weight, SOURCES[step])
        lanes_ref[8 * step : 8 * step + 8, :] = lanes
        for part in parts:
            weights_ref[8 * slot : 8 * slot + 8, :] = part
            slot += 1


def sweep_kernel(n, tm, message_slots, recv_ref, gram_ref, own_ref, lanes_ref, weights_ref, traces_ref, rms_ref):
    me = lax.axis_index("tile")
    half = lax.axis_index("tm")
    lane = iota((8, LANES), 1)
    block = lax.shift_right_logical(lane, 5)
    first = [tile_at(me, rel, n) * tm for rel in REACH]
    gram = gram_ref[...]

    def gathered(messages, group, turn):
        out = messages[4 * group]
        for q in range(4):
            if q or turn:
                out = jnp.where(block == (q + turn) % 4, messages[4 * group + q], out)
        return out

    def spare_of(messages, group, colour):
        return pltpu.roll(gathered(messages, group, 3), 64 if colour == 1 else 96, 1)

    def gram_of(spare, group, colour):
        rows = spread_row(spare, colour - 1)
        return jnp.where(block == colour, gram, rows) if group == 0 else rows

    def neighbours(step, tiles, spare, group, colour):
        slot = sum(len(sources) for sources in SOURCES[:step])
        total = None
        for i in range(8):
            at = jnp.broadcast_to(lanes_ref[8 * step + i : 8 * step + i + 1, :], (8, LANES))
            for s, tile in enumerate(tiles):
                place = 8 * (slot + s) + i
                weight = jnp.broadcast_to(weights_ref[place : place + 1, :], (8, LANES))
                if spare is not None and i >= LOW_SENT:
                    low = spread_row(spare, 2 * (i - LOW_SENT) + 1 + colour)
                    low = jnp.where(block == colour, 0.0, low) if group == 0 else low
                    weight = jnp.where(weight != 0.0, weight + low, 0.0)
                term = lookup(tile, at) * weight
                total = term if total is None else total + term
        return total

    energy, mine = None, None
    for t in range(tm):
        messages = [recv_ref[entry(message_slots, f + t)] for f in first]
        x0 = [gathered(messages, group, 0) for group in range(3)]
        x1 = []
        for group in range(2):
            spare = spare_of(messages, group, 1)
            fresh = gathered(messages, group, 1) - neighbours(group, x0[: 2 + group], spare, group, 1)
            x1.append(jnp.maximum(fresh / gram_of(spare, group, 1), 0.0))
        spare = spare_of(messages, 0, 2)
        fresh = gathered(messages, 0, 2) - neighbours(2, [x0[0], x0[1], x1[0], x1[1]], spare, 0, 2)
        x2 = jnp.maximum(fresh / gram_of(spare, 0, 2), 0.0)
        fresh = messages[0] - neighbours(3, [x0[0], x1[0], x2], None, 0, 3)
        x3 = jnp.maximum(fresh / gram, 0.0)
        own = pick([messages[0], x1[0], x2, x3], block)
        square = jnp.sum(own * own, axis=0, keepdims=True)
        energy = square if energy is None else energy + square
        mine = own if mine is None else jnp.where(half == t, own, mine)
    order = own_ref[16:24, :].astype(jnp.int32)
    traces_ref[...] = lookup(mine, order)
    energy = lookup(jnp.broadcast_to(energy, (8, LANES)), order)
    rms_ref[...] = jnp.sqrt(energy[0:1] / (8 * tm) + 1e-06)


def shards(
    data, send_list, footprint_slot, footprint, colour, correlation, correlation_gram, traces_init
):
    n = lax.axis_size("tile")
    tm = lax.axis_size("tm")
    tiles, devices = ORDERS.get((n, tm), (list(range(n)), list(range(n * tm))))
    f32, bf16 = jnp.float32, jnp.bfloat16
    shape = jax.ShapeDtypeStruct
    vmem = pl.BlockSpec(memory_space=pltpu.VMEM)
    hbm = pl.BlockSpec(memory_space=pltpu.HBM)

    def call(body, outs, ins, scratch=(), limit=VMEM_LIMIT):
        return pl.pallas_call(
            body,
            out_shape=outs,
            in_specs=ins,
            out_specs=[vmem] * len(outs),
            scratch_shapes=scratch,
            compiler_params=pltpu.CompilerParams(vmem_limit_bytes=limit),
        )

    inputs = (
        colour.reshape(1, LANES), correlation.T, correlation_gram.T, traces_init, footprint_slot.T,
        send_list[0].T, data,
    )
    outgoing, own = call(
        functools.partial(pack_kernel, n, slots_of(tiles)),
        [shape((n, DATA_ROWS + META_ROWS, LANES), bf16), shape((40, LANES), f32)],
        [hbm] * 7,
        [pltpu.VMEM(x.shape, x.dtype) for x in inputs[:5]]
        + [pltpu.SMEM(inputs[5].shape, jnp.int32), pltpu.VMEM(data.shape, bf16)]
        + [pltpu.SemaphoreType.DMA((7,))],
        PACK_LIMIT,
    )(*[pltpu.with_memory_space_constraint(x, pltpu.HBM) for x in inputs])
    arrived = lax.all_to_all(
        outgoing, "tile", split_axis=0, concat_axis=0, tiled=True, axis_index_groups=[tiles]
    )
    slots = sum(len(sources) for sources in SOURCES)
    message, gram, lanes, weights = call(
        functools.partial(project_kernel, n, tm, slots_of(tiles), slots_of(devices)),
        [shape((n * tm, 8, LANES), f32), shape((8, LANES), f32)]
        + [shape((8 * len(SOURCES), LANES), jnp.int32), shape((8 * slots, LANES), f32)],
        [vmem] * 3,
        [pltpu.VMEM((8 * LANES, LANES), f32)],
    )(arrived, footprint.reshape(8 * LANES, LANES), own)
    messages = lax.all_to_all(
        message, ("tile", "tm"), split_axis=0, concat_axis=0, tiled=True, axis_index_groups=[devices]
    )
    traces, rms = call(
        functools.partial(sweep_kernel, n, tm, slots_of(devices)),
        [shape((8, LANES), f32), shape((1, LANES), f32)],
        [vmem] * 5,
    )(messages, gram, own, lanes, weights)
    return (traces, rms.reshape(LANES))


def solution(mesh):
    placed = (
        P("tile", "tm", None),
        P("tile", None, None),
        P("tile", None),
        P("tile", None, None),
        P("tile"),
        P("tile", None),
        P("tile", None),
        P("tm", "tile"),
    )
    return jax.shard_map(
        shards, mesh=mesh, in_specs=placed, out_specs=(P("tm", "tile"), P("tile")), check_vma=False
    )
```

```python
import functools

import jax
import jax.numpy as jnp
from jax import lax
from jax.experimental import pallas as pl
from jax.experimental.pallas import tpu as pltpu
from jax.sharding import PartitionSpec as P

REACH = (
    (0, 0), (1, 0), (-1, 0), (0, 1),
    (1, 1), (-1, 1), (2, 0), (-2, 0),
    (3, 0), (-3, 0), (2, 1), (-2, 1),
)
NEAR = REACH[:4]
ORDERS = {
    (16, 2): (
        [11, 1, 14, 3, 12, 0, 10, 15, 7, 5, 13, 2, 6, 4, 8, 9],
        [0, 17, 26, 21, 1, 25, 7, 24, 29, 9, 16, 5, 22, 12, 18, 8]
        + [13, 20, 28, 14, 19, 3, 2, 4, 23, 31, 27, 10, 6, 11, 15, 30],
    ),
}
LANES = 128
QUARTER = 32
DATA_ROWS = 64
META_ROWS = 24
LOW_SENT = 6
GROUP = 4
VMEM_LIMIT = 48 * 2 ** 20
PACK_LIMIT = 48 * 2 ** 20
NT = (((1,), (1,)), ((), ()))


def iota(shape, dim):
    return lax.broadcasted_iota(jnp.int32, shape, dim)


def reach_at(device, near):
    return REACH.index((device[0] + near[0], (device[1] + near[1]) % 2))


def tile_at(me, rel, n):
    return lax.rem(me + rel[0] + rel[1] * (n // 2) + n, n)


def slots_of(order):
    return [order.index(device) for device in range(len(order))]


def entry(table, i):
    if table == list(range(len(table))):
        return i
    words = [sum(table[w + b] << (8 * b) for b in range(4)) for w in range(0, len(table), 4)]
    word, at = words[0], lax.shift_right_logical(i, 2)
    for w in range(1, len(words)):
        word = jnp.where(at == w, words[w], word)
    return jnp.bitwise_and(lax.shift_right_logical(word, 8 * jnp.bitwise_and(i, 3)), 255)


def dot(a, b):
    return jnp.dot(a, b, preferred_element_type=jnp.float32)


def dot_nt(a, b):
    return lax.dot_general(a, b, NT, preferred_element_type=jnp.float32)


def split2(x):
    hi = x.astype(jnp.bfloat16).astype(jnp.float32)
    return hi, x - hi


def split3(x):
    hi, rest = split2(x)
    mid, low = split2(rest)
    return jnp.concatenate([hi, mid, low], axis=0).astype(jnp.bfloat16)


def places(colour_row):
    in_class = colour_row == iota((8, LANES), 0)
    before = (iota((LANES, LANES), 0) < iota((LANES, LANES), 1)).astype(jnp.bfloat16)
    counts = dot(in_class.astype(jnp.bfloat16), before)
    rank = jnp.sum(jnp.where(in_class, counts, 0.0), axis=0, keepdims=True)
    return rank + (colour_row * QUARTER).astype(jnp.float32)


def pack_kernel(n, slots, *refs):
    sources, (out_ref, own_ref), held, sems = refs[:7], refs[7:9], refs[9:16], refs[16]
    colour_ref, corr_ref, gram_ref, init_ref, slot_ref, send_ref, data_ref = held
    copies = [pltpu.make_async_copy(a, b, sems.at[i]) for i, (a, b) in enumerate(zip(sources, held))]
    for copy in copies:
        copy.start()
    me = lax.axis_index("tile")
    lane = iota((8, LANES), 1)
    row = iota((8, LANES), 0)
    copies[0].wait()
    pos = places(colour_ref[...])
    order = (iota((LANES, LANES), 0).astype(jnp.float32) == pos).astype(jnp.bfloat16)
    for copy in copies[1:5]:
        copy.wait()
    own_ref[24:32, :] = slot_ref[...].astype(jnp.float32)
    ids = corr_ref[...]
    away = jnp.bitwise_and(lax.shift_right_logical(ids, 7) - me, n - 1)
    which = jnp.where(away == 0, 0, jnp.where(away == 1, 1, jnp.where(away == n - 1, 2, 3)))
    code = which * LANES + jnp.bitwise_and(ids, LANES - 1) - 2 * LANES
    code = code.astype(jnp.float32)
    gram = gram_ref[...]
    gram_hi, gram_lo = split2(gram)
    init_hi, init_lo = split2(init_ref[...])
    rows = [code, gram_hi, gram_lo, init_hi, init_lo, lane.astype(jnp.float32)]
    placed = dot_nt(jnp.concatenate(rows, axis=0).astype(jnp.bfloat16), order)
    placed = [placed[8 * i : 8 * i + 8] for i in range(6)]
    pos = jnp.broadcast_to(pos, (8, LANES))
    own_ref[0:8, :] = code
    own_ref[8:16, :] = gram
    own_ref[16:24, :] = pos
    own_ref[32:40, :] = placed[5]
    first = jnp.where(lane < 64, pltpu.roll(placed[0], 96, 1), pltpu.roll(placed[1], 32, 1))
    tails = []
    for low, even, odd in ((64, 96, 64), (32, 32, 0)):
        even = pltpu.roll(pos, even, 1)
        odd = pltpu.roll(pos, odd, 1) if odd else pos
        tails.append(
            jnp.where(row < LOW_SENT, pltpu.roll(placed[2], low, 1), jnp.where(row == LOW_SENT, even, odd))
        )
    second = jnp.where(lane < 96, pltpu.roll(placed[3], 96, 1), tails[0])
    third = jnp.where(lane < 96, pltpu.roll(placed[4], 96, 1), tails[1])
    meta = jnp.concatenate([first, second, third], axis=0)
    for copy in copies[5:]:
        copy.wait()
    for target in range(n):
        blocks = [data_ref[send_ref[c, target]].astype(jnp.float32) for c in range(8)]
        out_ref[slots[target]] = jnp.concatenate(blocks + [meta], axis=0).astype(jnp.bfloat16)


def column(row):
    eye = iota((LANES, LANES), 0) == iota((LANES, LANES), 1)
    return dot(jnp.where(eye, row, 0.0).astype(jnp.bfloat16), jnp.ones((LANES, LANES), jnp.bfloat16))


def lookup(table, index):
    return jnp.take_along_axis(table, index, axis=1, mode="promise_in_bounds")


def spread_row(rows, i):
    return jnp.broadcast_to(rows[i : i + 1], (8, LANES))


def pick(cases, which):
    out = cases[-1]
    for i in range(len(cases) - 1):
        out = jnp.where(which == i, cases[i], out)
    return out


def edges(devices, places_of, which, index, weight, sources):
    place, device = None, None
    for f in devices:
        found = lookup(places_of[f], index)
        place = found if place is None else jnp.where(which == f, found, place)
    place = place.astype(jnp.int32)
    colour = lax.shift_right_logical(place, 5)
    turn = jnp.bitwise_and(which + colour, 3)
    lanes = turn * QUARTER + jnp.bitwise_and(place, QUARTER - 1)
    tile = colour * 4 + lax.shift_right_logical(which, 2)
    return lanes, [jnp.where(tile == c * 4 + g, weight, 0.0) for c, g in sources]


SOURCES = (
    ((0, 0), (0, 1)),
    ((0, 0), (0, 1), (0, 2)),
    ((0, 0), (0, 1), (1, 0), (1, 1)),
    ((0, 0), (1, 0), (2, 0)),
)


def project_kernel(n, tm, slots, message_slots, recv_ref, fp_ref, own_ref, out_ref, gram_ref, lanes_ref, weights_ref, wide_ref):
    me = lax.axis_index("tile")
    lane = iota((8, LANES), 1)
    row = iota((8, LANES), 0)
    wide_ref[...] = fp_ref[...].astype(jnp.float32)
    weights, squares = [], None
    cut = 4 * n
    upper = (own_ref[24:32, :] >= float(cut)).astype(jnp.float32)
    for j in range(8):
        rows = wide_ref[pl.ds(j, LANES, stride=8), :]
        squares = rows * rows if j == 0 else squares + rows * rows
        above = column(upper[j : j + 1]) * rows
        weights.append(jnp.concatenate([rows - above, above], axis=1).astype(jnp.bfloat16))
    weights = jnp.concatenate(weights, axis=0)
    gram = dot_nt(jnp.ones((8, LANES), jnp.bfloat16), split3(squares))
    gram = gram[:, :LANES] + gram[:, LANES : 2 * LANES] + gram[:, 2 * LANES :]
    slot_rows = own_ref[24:32, :] - upper * float(cut)
    slot_row = jnp.concatenate([slot_rows[j : j + 1] for j in range(8)], axis=1)
    slot_row = jnp.broadcast_to(slot_row, (8, 8 * LANES))
    total = jnp.zeros((8, 8 * LANES), jnp.float32)
    for source in range(0, n // 2, GROUP):
        halves = []
        for first in (source, source + n // 2):
            blocks = [recv_ref[slots[first + i], :DATA_ROWS, :] for i in range(GROUP)]
            halves.append(jnp.concatenate(blocks, axis=0))
        product = dot_nt(jnp.concatenate(halves, axis=1), weights)
        for c in range(GROUP * 8):
            hit = slot_row == float(source * 8 + c)
            total = jnp.where(hit, product[8 * c : 8 * c + 8], total)
    projected = total[:, :LANES]
    for j in range(1, 8):
        projected = projected + total[:, j * LANES : (j + 1) * LANES]
    block = lax.shift_right_logical(lane, 5)
    metas = [recv_ref[entry(slots, tile_at(me, rel, n))].astype(jnp.float32)[DATA_ROWS:] for rel in REACH]
    places_of = []
    for meta in metas:
        parts = [spread_row(meta, 8 + LOW_SENT), spread_row(meta, 9 + LOW_SENT)]
        parts += [spread_row(meta, 16 + LOW_SENT), spread_row(meta, 17 + LOW_SENT)]
        parts = [pltpu.roll(part, 32 * i + 32, 1) if i < 3 else part for i, part in enumerate(parts)]
        places_of.append(pick(parts, block))
    code = own_ref[0:8, :].astype(jnp.int32) + 2 * LANES
    index, which = jnp.bitwise_and(code, LANES - 1), lax.shift_right_logical(code, 7)
    place = pick([lookup(places_of[r], index) for r in range(4)], which).astype(jnp.int32)
    own_place = own_ref[16:24, :].astype(jnp.int32)
    after = lax.shift_right_logical(place, 5) > lax.shift_right_logical(own_place, 5)
    late = jnp.where(after, own_ref[8:16, :], 0.0)
    starts = [pltpu.roll(meta[8:16] + meta[16:24], 32, 1) for meta in metas[:4]]
    held = None
    for i in range(8):
        at, owner = spread_row(place, i), spread_row(which, i)
        term = pick([lookup(start, at) for start in starts], owner) * spread_row(late, i)
        held = term if held is None else held + term
    names = own_ref[32:40, :].astype(jnp.int32)
    base = lookup(projected - held, names)
    gram = lookup(gram, names)
    gram_ref[...] = gram
    message = jnp.where(lane < QUARTER, jnp.maximum(base / gram, 0.0), base)
    listed = lookup(own_ref[8:16, :], names)
    rest = split2(listed)[1]
    spare = jnp.where(row < 4, spread_row(rest, LOW_SENT), spread_row(rest, LOW_SENT + 1))
    spare = jnp.where(row < 2, gram, spare)
    spare = jnp.where(jnp.bitwise_and(row, 1) == 0, pltpu.roll(spare, 64, 1), pltpu.roll(spare, 32, 1))
    others = jnp.where(lane < 96, message, spare)
    for t in range(n * tm):
        out_ref[t] = others
    for i, rel in enumerate(REACH):
        source = message if i == 0 else others
        turned = source if i % 4 == 0 else pltpu.roll(source, QUARTER * (i % 4), 1)
        target = tile_at(me, (-rel[0], rel[1]), n)
        for t in range(tm):
            out_ref[entry(message_slots, target * tm + t)] = turned
    codes = []
    for i in range(8):
        code = metas[i][0:8].astype(jnp.int32) + 2 * LANES
        at = [reach_at(REACH[i], near) for near in NEAR]
        device = pick(at, lax.shift_right_logical(code, 7))
        codes.append((device * LANES + jnp.bitwise_and(code, LANES - 1)).astype(jnp.float32))

    def gathered(parts, group, colour, start):
        out = None
        for q in range(4):
            p = (q + colour) % 4
            shift = (QUARTER * p - start) % LANES
            turned = parts[4 * group + q]
            turned = turned if shift == 0 else pltpu.roll(turned, shift, 1)
            out = turned if out is None else jnp.where(block == p, turned, out)
        return out

    high = [meta[0:8] for meta in metas[:8]]
    slot = 0
    for step, (group, colour) in enumerate(((0, 1), (1, 1), (0, 2), (0, 3))):
        if step < 3:
            start = QUARTER * (colour - 1)
            code = gathered(codes, group, colour, start).astype(jnp.int32)
            low = [jnp.where(row < LOW_SENT, meta[8 * colour : 8 * colour + 8], 0.0) for meta in metas[:8]]
            weight = gathered(high, group, colour, start + 64) + gathered(low, group, colour, 96)
            if group == 0:
                weight = jnp.where(block == colour, listed, weight)
            device, at = lax.shift_right_logical(code, 7), jnp.bitwise_and(code, LANES - 1)
            devices = range(12) if step == 1 else range(8)
        else:
            weight = listed
            device, at = lookup(which, names), lookup(index, names)
            devices = range(4)
        lanes, parts = edges(devices, places_of, device, at, weight, SOURCES[step])
        lanes_ref[8 * step : 8 * step + 8, :] = lanes
        for part in parts:
            weights_ref[8 * slot : 8 * slot + 8, :] = part
            slot += 1


def sweep_kernel(n, tm, message_slots, recv_ref, gram_ref, own_ref, lanes_ref, weights_ref, traces_ref, rms_ref):
    me = lax.axis_index("tile")
    half = lax.axis_index("tm")
    lane = iota((8, LANES), 1)
    block = lax.shift_right_logical(lane, 5)
    first = [tile_at(me, rel, n) * tm for rel in REACH]
    gram = gram_ref[...]

    def gathered(messages, group, turn):
        out = messages[4 * group]
        for q in range(4):
            if q or turn:
                out = jnp.where(block == (q + turn) % 4, messages[4 * group + q], out)
        return out

    def spare_of(messages, group, colour):
        return pltpu.roll(gathered(messages, group, 3), 64 if colour == 1 else 96, 1)

    def gram_of(spare, group, colour):
        rows = spread_row(spare, colour - 1)
        return jnp.where(block == colour, gram, rows) if group == 0 else rows

    def neighbours(step, tiles, spare, group, colour):
        slot = sum(len(sources) for sources in SOURCES[:step])
        total = None
        for i in range(8):
            at = jnp.broadcast_to(lanes_ref[8 * step + i : 8 * step + i + 1, :], (8, LANES))
            for s, tile in enumerate(tiles):
                place = 8 * (slot + s) + i
                weight = jnp.broadcast_to(weights_ref[place : place + 1, :], (8, LANES))
                if spare is not None and i >= LOW_SENT:
                    low = spread_row(spare, 2 * (i - LOW_SENT) + 1 + colour)
                    low = jnp.where(block == colour, 0.0, low) if group == 0 else low
                    weight = jnp.where(weight != 0.0, weight + low, 0.0)
                term = lookup(tile, at) * weight
                total = term if total is None else total + term
        return total

    energy, mine = None, None
    for t in range(tm):
        messages = [recv_ref[entry(message_slots, f + t)] for f in first]
        x0 = [gathered(messages, group, 0) for group in range(3)]
        x1 = []
        for group in range(2):
            spare = spare_of(messages, group, 1)
            fresh = gathered(messages, group, 1) - neighbours(group, x0[: 2 + group], spare, group, 1)
            x1.append(jnp.maximum(fresh / gram_of(spare, group, 1), 0.0))
        spare = spare_of(messages, 0, 2)
        fresh = gathered(messages, 0, 2) - neighbours(2, [x0[0], x0[1], x1[0], x1[1]], spare, 0, 2)
        x2 = jnp.maximum(fresh / gram_of(spare, 0, 2), 0.0)
        fresh = messages[0] - neighbours(3, [x0[0], x1[0], x2], None, 0, 3)
        x3 = jnp.maximum(fresh / gram, 0.0)
        own = pick([messages[0], x1[0], x2, x3], block)
        square = jnp.sum(own * own, axis=0, keepdims=True)
        energy = square if energy is None else energy + square
        mine = own if mine is None else jnp.where(half == t, own, mine)
    order = own_ref[16:24, :].astype(jnp.int32)
    traces_ref[...] = lookup(mine, order)
    energy = lookup(jnp.broadcast_to(energy, (8, LANES)), order)
    rms_ref[...] = jnp.sqrt(energy[0:1] / (8 * tm) + 1e-06)


def shards(
    data, send_list, footprint_slot, footprint, colour, correlation, correlation_gram, traces_init
):
    n = lax.axis_size("tile")
    tm = lax.axis_size("tm")
    tiles, devices = ORDERS.get((n, tm), (list(range(n)), list(range(n * tm))))
    f32, bf16 = jnp.float32, jnp.bfloat16
    shape = jax.ShapeDtypeStruct
    vmem = pl.BlockSpec(memory_space=pltpu.VMEM)
    hbm = pl.BlockSpec(memory_space=pltpu.HBM)

    def call(body, outs, ins, scratch=(), limit=VMEM_LIMIT):
        return pl.pallas_call(
            body,
            out_shape=outs,
            in_specs=ins,
            out_specs=[vmem] * len(outs),
            scratch_shapes=scratch,
            compiler_params=pltpu.CompilerParams(vmem_limit_bytes=limit),
        )

    inputs = (
        colour.reshape(1, LANES), correlation.T, correlation_gram.T, traces_init, footprint_slot.T,
        send_list[0].T, data,
    )
    outgoing, own = call(
        functools.partial(pack_kernel, n, slots_of(tiles)),
        [shape((n, DATA_ROWS + META_ROWS, LANES), bf16), shape((40, LANES), f32)],
        [hbm] * 7,
        [pltpu.VMEM(x.shape, x.dtype) for x in inputs[:5]]
        + [pltpu.SMEM(inputs[5].shape, jnp.int32), pltpu.VMEM(data.shape, bf16)]
        + [pltpu.SemaphoreType.DMA((7,))],
        PACK_LIMIT,
    )(*[pltpu.with_memory_space_constraint(x, pltpu.HBM) for x in inputs])
    arrived = lax.all_to_all(
        outgoing, "tile", split_axis=0, concat_axis=0, tiled=True, axis_index_groups=[tiles]
    )
    slots = sum(len(sources) for sources in SOURCES)
    message, gram, lanes, weights = call(
        functools.partial(project_kernel, n, tm, slots_of(tiles), slots_of(devices)),
        [shape((n * tm, 8, LANES), f32), shape((8, LANES), f32)]
        + [shape((8 * len(SOURCES), LANES), jnp.int32), shape((8 * slots, LANES), f32)],
        [vmem] * 3,
        [pltpu.VMEM((8 * LANES, LANES), f32)],
    )(arrived, footprint.reshape(8 * LANES, LANES), own)
    messages = lax.all_to_all(
        message, ("tile", "tm"), split_axis=0, concat_axis=0, tiled=True, axis_index_groups=[devices]
    )
    traces, rms = call(
        functools.partial(sweep_kernel, n, tm, slots_of(devices)),
        [shape((8, LANES), f32), shape((1, LANES), f32)],
        [vmem] * 5,
    )(messages, gram, own, lanes, weights)
    return (traces, rms.reshape(LANES))


def solution(mesh):
    placed = (
        P("tile", "tm", None),
        P("tile", None, None),
        P("tile", None),
        P("tile", None, None),
        P("tile"),
        P("tile", None),
        P("tile", None),
        P("tm", "tile"),
    )
    return jax.shard_map(
        shards, mesh=mesh, in_specs=placed, out_specs=(P("tm", "tile"), P("tile")), check_vma=False
    )
```

```python
import functools

import jax
import jax.numpy as jnp
from jax import lax
from jax.experimental import pallas as pl
from jax.experimental.pallas import tpu as pltpu
from jax.sharding import PartitionSpec as P

REACH = (
    (0, 0), (1, 0), (-1, 0), (0, 1),
    (1, 1), (-1, 1), (2, 0), (-2, 0),
    (3, 0), (-3, 0), (2, 1), (-2, 1),
)
NEAR = REACH[:4]
ORDERS = {
    (16, 2): (
        [11, 1, 14, 3, 12, 0, 10, 15, 7, 5, 13, 2, 6, 4, 8, 9],
        [0, 17, 26, 21, 1, 25, 7, 24, 29, 9, 16, 5, 22, 12, 18, 8]
        + [13, 20, 28, 14, 19, 3, 2, 4, 23, 31, 27, 10, 6, 11, 15, 30],
    ),
}
LANES = 128
QUARTER = 32
DATA_ROWS = 64
META_ROWS = 24
LOW_SENT = 6
GROUP = 8
VMEM_LIMIT = 48 * 2 ** 20
PACK_LIMIT = 48 * 2 ** 20
NT = (((1,), (1,)), ((), ()))


def iota(shape, dim):
    return lax.broadcasted_iota(jnp.int32, shape, dim)


def reach_at(device, near):
    return REACH.index((device[0] + near[0], (device[1] + near[1]) % 2))


def tile_at(me, rel, n):
    return lax.rem(me + rel[0] + rel[1] * (n // 2) + n, n)


def slots_of(order):
    return [order.index(device) for device in range(len(order))]


def entry(table, i):
    if table == list(range(len(table))):
        return i
    words = [sum(table[w + b] << (8 * b) for b in range(4)) for w in range(0, len(table), 4)]
    word, at = words[0], lax.shift_right_logical(i, 2)
    for w in range(1, len(words)):
        word = jnp.where(at == w, words[w], word)
    return jnp.bitwise_and(lax.shift_right_logical(word, 8 * jnp.bitwise_and(i, 3)), 255)


def dot(a, b):
    return jnp.dot(a, b, preferred_element_type=jnp.float32)


def dot_nt(a, b):
    return lax.dot_general(a, b, NT, preferred_element_type=jnp.float32)


def split2(x):
    hi = x.astype(jnp.bfloat16).astype(jnp.float32)
    return hi, x - hi


def split3(x):
    hi, rest = split2(x)
    mid, low = split2(rest)
    return jnp.concatenate([hi, mid, low], axis=0).astype(jnp.bfloat16)


def places(colour_row):
    in_class = colour_row == iota((8, LANES), 0)
    before = (iota((LANES, LANES), 0) < iota((LANES, LANES), 1)).astype(jnp.bfloat16)
    counts = dot(in_class.astype(jnp.bfloat16), before)
    rank = jnp.sum(jnp.where(in_class, counts, 0.0), axis=0, keepdims=True)
    return rank + (colour_row * QUARTER).astype(jnp.float32)


def pack_kernel(n, slots, *refs):
    sources, (out_ref, own_ref), held, sems = refs[:7], refs[7:9], refs[9:16], refs[16]
    colour_ref, corr_ref, gram_ref, init_ref, slot_ref, send_ref, data_ref = held
    copies = [pltpu.make_async_copy(a, b, sems.at[i]) for i, (a, b) in enumerate(zip(sources, held))]
    for copy in copies:
        copy.start()
    me = lax.axis_index("tile")
    lane = iota((8, LANES), 1)
    row = iota((8, LANES), 0)
    copies[0].wait()
    pos = places(colour_ref[...])
    order = (iota((LANES, LANES), 0).astype(jnp.float32) == pos).astype(jnp.bfloat16)
    for copy in copies[1:5]:
        copy.wait()
    own_ref[24:32, :] = slot_ref[...].astype(jnp.float32)
    ids = corr_ref[...]
    away = jnp.bitwise_and(lax.shift_right_logical(ids, 7) - me, n - 1)
    which = jnp.where(away == 0, 0, jnp.where(away == 1, 1, jnp.where(away == n - 1, 2, 3)))
    code = which * LANES + jnp.bitwise_and(ids, LANES - 1) - 2 * LANES
    code = code.astype(jnp.float32)
    gram = gram_ref[...]
    gram_hi, gram_lo = split2(gram)
    init_hi, init_lo = split2(init_ref[...])
    rows = [code, gram_hi, gram_lo, init_hi, init_lo, lane.astype(jnp.float32)]
    placed = dot_nt(jnp.concatenate(rows, axis=0).astype(jnp.bfloat16), order)
    placed = [placed[8 * i : 8 * i + 8] for i in range(6)]
    pos = jnp.broadcast_to(pos, (8, LANES))
    own_ref[0:8, :] = code
    own_ref[8:16, :] = gram
    own_ref[16:24, :] = pos
    own_ref[32:40, :] = placed[5]
    first = jnp.where(lane < 64, pltpu.roll(placed[0], 96, 1), pltpu.roll(placed[1], 32, 1))
    tails = []
    for low, even, odd in ((64, 96, 64), (32, 32, 0)):
        even = pltpu.roll(pos, even, 1)
        odd = pltpu.roll(pos, odd, 1) if odd else pos
        tails.append(
            jnp.where(row < LOW_SENT, pltpu.roll(placed[2], low, 1), jnp.where(row == LOW_SENT, even, odd))
        )
    second = jnp.where(lane < 96, pltpu.roll(placed[3], 96, 1), tails[0])
    third = jnp.where(lane < 96, pltpu.roll(placed[4], 96, 1), tails[1])
    meta = jnp.concatenate([first, second, third], axis=0)
    for copy in copies[5:]:
        copy.wait()
    for target in range(n):
        blocks = [data_ref[send_ref[c, target]].astype(jnp.float32) for c in range(8)]
        out_ref[slots[target]] = jnp.concatenate(blocks + [meta], axis=0).astype(jnp.bfloat16)


def column(row):
    eye = iota((LANES, LANES), 0) == iota((LANES, LANES), 1)
    return dot(jnp.where(eye, row, 0.0).astype(jnp.bfloat16), jnp.ones((LANES, LANES), jnp.bfloat16))


def lookup(table, index):
    return jnp.take_along_axis(table, index, axis=1, mode="promise_in_bounds")


def spread_row(rows, i):
    return jnp.broadcast_to(rows[i : i + 1], (8, LANES))


def pick(cases, which):
    out = cases[-1]
    for i in range(len(cases) - 1):
        out = jnp.where(which == i, cases[i], out)
    return out


def edges(devices, places_of, which, index, weight, sources):
    place, device = None, None
    for f in devices:
        found = lookup(places_of[f], index)
        place = found if place is None else jnp.where(which == f, found, place)
    place = place.astype(jnp.int32)
    colour = lax.shift_right_logical(place, 5)
    turn = jnp.bitwise_and(which + colour, 3)
    lanes = turn * QUARTER + jnp.bitwise_and(place, QUARTER - 1)
    tile = colour * 4 + lax.shift_right_logical(which, 2)
    return lanes, [jnp.where(tile == c * 4 + g, weight, 0.0) for c, g in sources]


SOURCES = (
    ((0, 0), (0, 1)),
    ((0, 0), (0, 1), (0, 2)),
    ((0, 0), (0, 1), (1, 0), (1, 1)),
    ((0, 0), (1, 0), (2, 0)),
)


def project_kernel(n, tm, slots, message_slots, recv_ref, fp_ref, own_ref, out_ref, gram_ref, lanes_ref, weights_ref, wide_ref):
    me = lax.axis_index("tile")
    lane = iota((8, LANES), 1)
    row = iota((8, LANES), 0)
    wide_ref[...] = fp_ref[...].astype(jnp.float32)
    weights, squares = [], None
    cut = 4 * n
    upper = (own_ref[24:32, :] >= float(cut)).astype(jnp.float32)
    for j in range(8):
        rows = wide_ref[pl.ds(j, LANES, stride=8), :]
        squares = rows * rows if j == 0 else squares + rows * rows
        above = column(upper[j : j + 1]) * rows
        weights.append(jnp.concatenate([rows - above, above], axis=1).astype(jnp.bfloat16))
    weights = jnp.concatenate(weights, axis=0)
    gram = dot_nt(jnp.ones((8, LANES), jnp.bfloat16), split3(squares))
    gram = gram[:, :LANES] + gram[:, LANES : 2 * LANES] + gram[:, 2 * LANES :]
    slot_rows = own_ref[24:32, :] - upper * float(cut)
    slot_row = jnp.concatenate([slot_rows[j : j + 1] for j in range(8)], axis=1)
    slot_row = jnp.broadcast_to(slot_row, (8, 8 * LANES))
    total = jnp.zeros((8, 8 * LANES), jnp.float32)
    for source in range(0, n // 2, GROUP):
        halves = []
        for first in (source, source + n // 2):
            blocks = [recv_ref[slots[first + i], :DATA_ROWS, :] for i in range(GROUP)]
            halves.append(jnp.concatenate(blocks, axis=0))
        product = dot_nt(jnp.concatenate(halves, axis=1), weights)
        for c in range(GROUP * 8):
            hit = slot_row == float(source * 8 + c)
            total = jnp.where(hit, product[8 * c : 8 * c + 8], total)
    projected = total[:, :LANES]
    for j in range(1, 8):
        projected = projected + total[:, j * LANES : (j + 1) * LANES]
    block = lax.shift_right_logical(lane, 5)
    metas = [recv_ref[entry(slots, tile_at(me, rel, n))].astype(jnp.float32)[DATA_ROWS:] for rel in REACH]
    places_of = []
    for meta in metas:
        parts = [spread_row(meta, 8 + LOW_SENT), spread_row(meta, 9 + LOW_SENT)]
        parts += [spread_row(meta, 16 + LOW_SENT), spread_row(meta, 17 + LOW_SENT)]
        parts = [pltpu.roll(part, 32 * i + 32, 1) if i < 3 else part for i, part in enumerate(parts)]
        places_of.append(pick(parts, block))
    code = own_ref[0:8, :].astype(jnp.int32) + 2 * LANES
    index, which = jnp.bitwise_and(code, LANES - 1), lax.shift_right_logical(code, 7)
    place = pick([lookup(places_of[r], index) for r in range(4)], which).astype(jnp.int32)
    own_place = own_ref[16:24, :].astype(jnp.int32)
    after = lax.shift_right_logical(place, 5) > lax.shift_right_logical(own_place, 5)
    late = jnp.where(after, own_ref[8:16, :], 0.0)
    starts = [pltpu.roll(meta[8:16] + meta[16:24], 32, 1) for meta in metas[:4]]
    held = None
    for i in range(8):
        at, owner = spread_row(place, i), spread_row(which, i)
        term = pick([lookup(start, at) for start in starts], owner) * spread_row(late, i)
        held = term if held is None else held + term
    names = own_ref[32:40, :].astype(jnp.int32)
    base = lookup(projected - held, names)
    gram = lookup(gram, names)
    gram_ref[...] = gram
    message = jnp.where(lane < QUARTER, jnp.maximum(base / gram, 0.0), base)
    listed = lookup(own_ref[8:16, :], names)
    rest = split2(listed)[1]
    spare = jnp.where(row < 4, spread_row(rest, LOW_SENT), spread_row(rest, LOW_SENT + 1))
    spare = jnp.where(row < 2, gram, spare)
    spare = jnp.where(jnp.bitwise_and(row, 1) == 0, pltpu.roll(spare, 64, 1), pltpu.roll(spare, 32, 1))
    others = jnp.where(lane < 96, message, spare)
    for t in range(n * tm):
        out_ref[t] = others
    for i, rel in enumerate(REACH):
        source = message if i == 0 else others
        turned = source if i % 4 == 0 else pltpu.roll(source, QUARTER * (i % 4), 1)
        target = tile_at(me, (-rel[0], rel[1]), n)
        for t in range(tm):
            out_ref[entry(message_slots, target * tm + t)] = turned
    codes = []
    for i in range(8):
        code = metas[i][0:8].astype(jnp.int32) + 2 * LANES
        at = [reach_at(REACH[i], near) for near in NEAR]
        device = pick(at, lax.shift_right_logical(code, 7))
        codes.append((device * LANES + jnp.bitwise_and(code, LANES - 1)).astype(jnp.float32))

    def gathered(parts, group, colour, start):
        out = None
        for q in range(4):
            p = (q + colour) % 4
            shift = (QUARTER * p - start) % LANES
            turned = parts[4 * group + q]
            turned = turned if shift == 0 else pltpu.roll(turned, shift, 1)
            out = turned if out is None else jnp.where(block == p, turned, out)
        return out

    high = [meta[0:8] for meta in metas[:8]]
    slot = 0
    for step, (group, colour) in enumerate(((0, 1), (1, 1), (0, 2), (0, 3))):
        if step < 3:
            start = QUARTER * (colour - 1)
            code = gathered(codes, group, colour, start).astype(jnp.int32)
            low = [jnp.where(row < LOW_SENT, meta[8 * colour : 8 * colour + 8], 0.0) for meta in metas[:8]]
            weight = gathered(high, group, colour, start + 64) + gathered(low, group, colour, 96)
            if group == 0:
                weight = jnp.where(block == colour, listed, weight)
            device, at = lax.shift_right_logical(code, 7), jnp.bitwise_and(code, LANES - 1)
            devices = range(12) if step == 1 else range(8)
        else:
            weight = listed
            device, at = lookup(which, names), lookup(index, names)
            devices = range(4)
        lanes, parts = edges(devices, places_of, device, at, weight, SOURCES[step])
        lanes_ref[8 * step : 8 * step + 8, :] = lanes
        for part in parts:
            weights_ref[8 * slot : 8 * slot + 8, :] = part
            slot += 1


def sweep_kernel(n, tm, message_slots, recv_ref, gram_ref, own_ref, lanes_ref, weights_ref, traces_ref, rms_ref):
    me = lax.axis_index("tile")
    half = lax.axis_index("tm")
    lane = iota((8, LANES), 1)
    block = lax.shift_right_logical(lane, 5)
    first = [tile_at(me, rel, n) * tm for rel in REACH]
    gram = gram_ref[...]

    def gathered(messages, group, turn):
        out = messages[4 * group]
        for q in range(4):
            if q or turn:
                out = jnp.where(block == (q + turn) % 4, messages[4 * group + q], out)
        return out

    def spare_of(messages, group, colour):
        return pltpu.roll(gathered(messages, group, 3), 64 if colour == 1 else 96, 1)

    def gram_of(spare, group, colour):
        rows = spread_row(spare, colour - 1)
        return jnp.where(block == colour, gram, rows) if group == 0 else rows

    def neighbours(step, tiles, spare, group, colour):
        slot = sum(len(sources) for sources in SOURCES[:step])
        total = None
        for i in range(8):
            at = jnp.broadcast_to(lanes_ref[8 * step + i : 8 * step + i + 1, :], (8, LANES))
            for s, tile in enumerate(tiles):
                place = 8 * (slot + s) + i
                weight = jnp.broadcast_to(weights_ref[place : place + 1, :], (8, LANES))
                if spare is not None and i >= LOW_SENT:
                    low = spread_row(spare, 2 * (i - LOW_SENT) + 1 + colour)
                    low = jnp.where(block == colour, 0.0, low) if group == 0 else low
                    weight = jnp.where(weight != 0.0, weight + low, 0.0)
                term = lookup(tile, at) * weight
                total = term if total is None else total + term
        return total

    energy, mine = None, None
    for t in range(tm):
        messages = [recv_ref[entry(message_slots, f + t)] for f in first]
        x0 = [gathered(messages, group, 0) for group in range(3)]
        x1 = []
        for group in range(2):
            spare = spare_of(messages, group, 1)
            fresh = gathered(messages, group, 1) - neighbours(group, x0[: 2 + group], spare, group, 1)
            x1.append(jnp.maximum(fresh / gram_of(spare, group, 1), 0.0))
        spare = spare_of(messages, 0, 2)
        fresh = gathered(messages, 0, 2) - neighbours(2, [x0[0], x0[1], x1[0], x1[1]], spare, 0, 2)
        x2 = jnp.maximum(fresh / gram_of(spare, 0, 2), 0.0)
        fresh = messages[0] - neighbours(3, [x0[0], x1[0], x2], None, 0, 3)
        x3 = jnp.maximum(fresh / gram, 0.0)
        own = pick([messages[0], x1[0], x2, x3], block)
        square = jnp.sum(own * own, axis=0, keepdims=True)
        energy = square if energy is None else energy + square
        mine = own if mine is None else jnp.where(half == t, own, mine)
    order = own_ref[16:24, :].astype(jnp.int32)
    traces_ref[...] = lookup(mine, order)
    energy = lookup(jnp.broadcast_to(energy, (8, LANES)), order)
    rms_ref[...] = jnp.sqrt(energy[0:1] / (8 * tm) + 1e-06)


def shards(
    data, send_list, footprint_slot, footprint, colour, correlation, correlation_gram, traces_init
):
    n = lax.axis_size("tile")
    tm = lax.axis_size("tm")
    tiles, devices = ORDERS.get((n, tm), (list(range(n)), list(range(n * tm))))
    f32, bf16 = jnp.float32, jnp.bfloat16
    shape = jax.ShapeDtypeStruct
    vmem = pl.BlockSpec(memory_space=pltpu.VMEM)
    hbm = pl.BlockSpec(memory_space=pltpu.HBM)

    def call(body, outs, ins, scratch=(), limit=VMEM_LIMIT):
        return pl.pallas_call(
            body,
            out_shape=outs,
            in_specs=ins,
            out_specs=[vmem] * len(outs),
            scratch_shapes=scratch,
            compiler_params=pltpu.CompilerParams(vmem_limit_bytes=limit),
        )

    inputs = (
        colour.reshape(1, LANES), correlation.T, correlation_gram.T, traces_init, footprint_slot.T,
        send_list[0].T, data,
    )
    outgoing, own = call(
        functools.partial(pack_kernel, n, slots_of(tiles)),
        [shape((n, DATA_ROWS + META_ROWS, LANES), bf16), shape((40, LANES), f32)],
        [hbm] * 7,
        [pltpu.VMEM(x.shape, x.dtype) for x in inputs[:5]]
        + [pltpu.SMEM(inputs[5].shape, jnp.int32), pltpu.VMEM(data.shape, bf16)]
        + [pltpu.SemaphoreType.DMA((7,))],
        PACK_LIMIT,
    )(*[pltpu.with_memory_space_constraint(x, pltpu.HBM) for x in inputs])
    arrived = lax.all_to_all(
        outgoing, "tile", split_axis=0, concat_axis=0, tiled=True, axis_index_groups=[tiles]
    )
    slots = sum(len(sources) for sources in SOURCES)
    message, gram, lanes, weights = call(
        functools.partial(project_kernel, n, tm, slots_of(tiles), slots_of(devices)),
        [shape((n * tm, 8, LANES), f32), shape((8, LANES), f32)]
        + [shape((8 * len(SOURCES), LANES), jnp.int32), shape((8 * slots, LANES), f32)],
        [vmem] * 3,
        [pltpu.VMEM((8 * LANES, LANES), f32)],
    )(arrived, footprint.reshape(8 * LANES, LANES), own)
    messages = lax.all_to_all(
        message, ("tile", "tm"), split_axis=0, concat_axis=0, tiled=True, axis_index_groups=[devices]
    )
    traces, rms = call(
        functools.partial(sweep_kernel, n, tm, slots_of(devices)),
        [shape((8, LANES), f32), shape((1, LANES), f32)],
        [vmem] * 5,
    )(messages, gram, own, lanes, weights)
    return (traces, rms.reshape(LANES))


def solution(mesh):
    placed = (
        P("tile", "tm", None),
        P("tile", None, None),
        P("tile", None),
        P("tile", None, None),
        P("tile"),
        P("tile", None),
        P("tile", None),
        P("tm", "tile"),
    )
    return jax.shard_map(
        shards, mesh=mesh, in_specs=placed, out_specs=(P("tm", "tile"), P("tile")), check_vma=False
    )
```
